32 devices in a mesh: groups: 2 (over x), context: 16 (over z, y, core).
Axes of the slice: x: 2, y: 2, z: 4, core: 2. Of those that a mesh axis runs over, the one named last changes fastest.
Arguments:
- xbc_raw: bfloat16 [4096, 3712], P(('groups', 'context')), parts along dimension 0, may hold values from -6 to 6
- gate_z: bfloat16 [4096, 3584], P(('groups', 'context')), parts along dimension 0, may hold values from -6 to 6
- dt_raw: float32 [4096, 56], P(('groups', 'context')), parts along dimension 0, may hold values from -5 to 5
- a_log: float32 [56], replicated, may hold values from -16 to -2
- conv_weight: float32 [4, 3712], replicated, may hold values from -3 to 3
- norm_gain: float32 [3584], replicated, may hold values from 0.1 to 1.9
- grad_out: bfloat16 [4096, 3584], P(('groups', 'context')), parts along dimension 0, may hold values from -6 to 6
Outputs:
- normed: bfloat16 [4096, 3584], P(('groups', 'context')), parts along dimension 0
- grad_xbc: bfloat16 [4096, 3712], P(('groups', 'context')), parts along dimension 0
- grad_z: bfloat16 [4096, 3584], P(('groups', 'context')), parts along dimension 0
- grad_dt: float32 [4096, 56], P(('groups', 'context')), parts along dimension 0
- grad_conv: float32 [8, 3712], P('groups'), parts along dimension 0
- grad_alog: float32 [112], P('groups'), parts along dimension 0
- grad_gain: float32 [7168], P('groups'), parts along dimension 0
The draws below stay inside these ranges and needn't reach their ends.
There are 2 independent parts, one for each index of `groups`. The reference program is written for one: setup_inputs(seed, part) draws one part's arguments, and reference() takes and returns one part's arrays. A program takes and returns all parts, laid end to end along the dimension named above; an argument that names none is the same for every part. Nothing has to cross between parts.
All inputs are finite; a program needn't handle non-finite values.
Results may differ from the reference program's by a relative error of at most 0.0085.
The reference program's roundings to bfloat16 on the way count: a program that leaves them out, or rounds other values in their place, can miss the bound.
Values may be sent and summed in bfloat16 or wider, within the bound.
A program may use at most 128 MiB of HBM per device.

```python
import math
import jax
import jax.numpy as jnp
from jax import lax

HEADS = 56
HEADDIM = 64
DSTATE = 64
KERNEL = 4
TOK_DEV = 128
INNER = 3584
CH = 3712
TOKENS = 2048


def head_rates(key, slow_share):
    pick_key, fast_key, slow_key = jax.random.split(key, 3)
    slow_heads = jax.random.uniform(pick_key, (HEADS,)) < slow_share
    fast_rate = jnp.exp(jax.random.uniform(fast_key, (HEADS,), minval=math.log(1.0 / 50.0), maxval=math.log(1.0 / 25.0)))
    slow_rate = jnp.exp(jax.random.uniform(slow_key, (HEADS,), minval=math.log(0.15), maxval=math.log(0.6))) / TOKENS
    chosen = jnp.where(slow_heads, slow_rate, fast_rate)
    return jnp.log(chosen / 0.8).astype(jnp.float32)


def draw_a_log(key, part):
    key = jax.random.fold_in(key, 7)
    slow_share = 0.5
    return head_rates(key, slow_share)


def block_scale(own_key, dims, cuts, smallest, largest):
    def one(position, shards_of):
        steps = jax.random.uniform(jax.random.fold_in(jax.random.fold_in(own_key, 6), position), (shards_of,), jnp.float32, smallest / len(cuts), largest / len(cuts))
        return jnp.repeat(jnp.exp(steps), dims[position] // shards_of).reshape((-1,) + (1,) * (len(dims) - position - 1))

    loudness = one(*cuts[0])
    for cut in cuts[1:]:
        loudness = loudness * one(*cut)
    return loudness


def noise(key, dims, deviation, limit, cuts=(), held_as=jnp.bfloat16):
    result = deviation * jax.random.normal(key, dims, jnp.float32)
    if cuts:
        result = result * block_scale(key, dims, cuts, -0.22, 0.18)
    return jnp.clip(result, -limit, limit).astype(held_as)


def setup_inputs(seed: int = 0, part: int = 0) -> dict:
    splits = jax.random.split(jax.random.key(seed), 8)
    part_splits = jax.random.split(jax.random.fold_in(splits[7], part), 8)
    return {
        "xbc_raw": noise(part_splits[0], (TOKENS, CH), 1.0, 6.0, ((0, 16),)),
        "gate_z": noise(part_splits[1], (TOKENS, INNER), 1.0, 6.0, ((0, 16),)),
        "dt_raw": noise(part_splits[2], (TOKENS, HEADS), 1.0, 5.0, ((0, 16),), jnp.float32),
        "a_log": draw_a_log(jax.random.fold_in(splits[7], 71), part),
        "conv_weight": noise(splits[4], (KERNEL, CH), KERNEL ** -0.5, 3.0, (), jnp.float32),
        "norm_gain": jnp.clip(1.0 + 0.18 * jax.random.normal(splits[5], (INNER,), jnp.float32), 0.1, 1.9),
        "grad_out": noise(part_splits[6], (TOKENS, INNER), 1.0, 6.0, ((0, 16),)),
    }


def conv_silu(extended, conv_weight):
    taps = conv_weight.shape[0]
    out_rows = extended.shape[0] - taps + 1
    summed = jnp.zeros((out_rows, extended.shape[1]), jnp.float32)
    for offset in range(taps):
        summed = summed + conv_weight[offset][None, :] * extended[offset:offset + out_rows]
    return jax.nn.silu(summed).astype(jnp.bfloat16)

def local_part(inputs, dt_piece, a_log):
    length = inputs.shape[0]
    values = inputs[:, :INNER].reshape(length, HEADS, HEADDIM)
    b_proj = inputs[:, INNER:INNER + DSTATE]
    c_proj = inputs[:, INNER + DSTATE:]
    step_size = jax.nn.softplus(dt_piece)
    log_decay = -jnp.exp(a_log)[None, :] * step_size
    running = jnp.cumsum(log_decay, axis=0)
    scores = jnp.dot(c_proj, b_proj.T, precision=lax.Precision.HIGHEST)
    causal = (jnp.arange(length)[:, None] >= jnp.arange(length)[None, :])[None, :, :]
    run_heads = running.T
    log_gap = run_heads[:, :, None] - run_heads[:, None, :]
    decays = jnp.where(causal, jnp.exp(jnp.where(causal, log_gap, 0.0)), 0.0)
    weights = scores[None, :, :] * decays * step_size.T[:, None, :]
    intra_out = jnp.einsum('hts,shp->thp', weights, values, precision=lax.Precision.HIGHEST)
    to_end = jnp.exp(running[-1][None, :] - running) * step_size
    end_state = jnp.einsum('thp,tn->hpn', values * to_end[:, :, None], b_proj, precision=lax.Precision.HIGHEST)
    return (intra_out, end_state, running[-1], running)

def inter_part(start_state, running, inputs):
    c_proj = inputs[:, INNER + DSTATE:]
    carried = jnp.einsum('hpn,tn->thp', start_state, c_proj, precision=lax.Precision.HIGHEST)
    return carried * jnp.exp(running)[:, :, None]

def gated_norm(mixer_out, gate_in, gain_in):
    gated = mixer_out * jax.nn.silu(gate_in.astype(jnp.float32))
    scale = lax.rsqrt(lax.optimization_barrier(jnp.mean(gated * gated, axis=-1, keepdims=True)) + 1e-05)
    return gated * scale * gain_in

def reference(xbc_raw, gate_z, dt_raw, a_log, conv_weight, norm_gain, grad_out):

    def forward(xbc_in, gate_in, dt_in, alog_in, conv_in, gain_in):
        zero_rows = jnp.zeros((KERNEL - 1, CH), jnp.bfloat16)
        extended = jnp.concatenate([zero_rows, xbc_in], axis=0).astype(jnp.float32)
        mixin = conv_silu(extended, conv_in)
        inputs = lax.optimization_barrier(mixin).astype(jnp.float32)
        blocks = TOKENS // TOK_DEV
        input_blocks = inputs.reshape(blocks, TOK_DEV, CH)
        dt_blocks = dt_in.reshape(blocks, TOK_DEV, HEADS)

        def advance(state_now, pieces):
            input_piece, dt_piece = pieces
            intra_out, end_state, block_total, running = local_part(input_piece, dt_piece, alog_in)
            block_out = intra_out + inter_part(state_now, running, input_piece)
            state_next = jnp.exp(block_total)[:, None, None] * state_now + end_state
            return (state_next, block_out)
        start_zero = jnp.zeros((HEADS, HEADDIM, DSTATE), jnp.float32)
        _, outputs = lax.scan(jax.checkpoint(advance), start_zero, (input_blocks, dt_blocks))
        mixer = outputs.reshape(TOKENS, INNER)
        return gated_norm(mixer, gate_in, gain_in)
    normed, pullback = jax.vjp(forward, xbc_raw, gate_z, dt_raw, a_log, conv_weight, norm_gain)
    cotangents = pullback(grad_out.astype(jnp.float32))
    return (normed.astype(jnp.bfloat16), cotangents[0], cotangents[1], cotangents[2], cotangents[4], cotangents[3], cotangents[5])
```

```python
import functools
import math

import jax
import jax.numpy as jnp
from jax import lax
from jax.experimental import pallas as pl
from jax.experimental.pallas import tpu as pltpu
from jax.sharding import PartitionSpec as P

HEADDIM = 64
DSTATE = 64
LANES = 128
MESH = pl.DeviceIdType.MESH
F32 = jnp.float32
BF16 = jnp.bfloat16
VMEM_LIMIT = 48 * 1024 * 1024


def dot(a, b, ca=1, cb=0):
    return lax.dot_general(a, b, (((ca,), (cb,)), ((), ())), preferred_element_type=F32)


def dot_exact(a, b):
    return jnp.dot(a, b, precision=lax.Precision.HIGHEST, preferred_element_type=F32)


def iota(shape, axis):
    return lax.broadcasted_iota(jnp.int32, shape, axis)


def tile_at(k):
    return pl.ds(pl.multiple_of(k * LANES, LANES), LANES)


def conv_pre(x, halo, taps):
    ext = jnp.concatenate([halo, x], axis=0)
    rows = x.shape[0]
    return ext, sum(taps[o : o + 1] * ext[5 + o : 5 + o + rows] for o in range(4))


def sigmoid(v):
    return 1.0 / (1.0 + jnp.exp(-v))


def steps_of(dt_ref, alog_ref, run_t, step_t):
    raw = dt_ref[...]
    step = jnp.maximum(raw, 0.0) + jnp.log1p(jnp.exp(-jnp.abs(raw)))
    log_decay = -jnp.exp(alog_ref[0:1]) * step
    rows = raw.shape[0]
    tri = (iota((rows, rows), 0) >= iota((rows, rows), 1)).astype(F32)
    running = dot_exact(tri, log_decay)
    run_t[...] = running.T
    step_t[...] = step.T
    return step, log_decay, running


def columns_of(row_ref, k):
    low = jnp.broadcast_to(row_ref[pl.ds(2 * k, 1), :], (LANES, LANES))
    high = jnp.broadcast_to(row_ref[pl.ds(2 * k + 1, 1), :], (LANES, LANES))
    low_t, high_t = low.T, high.T
    return low, high, low_t, high_t, jnp.where(iota((LANES, LANES), 1) < HEADDIM, low_t, high_t)


def pair_weights(run_t, step_t, k):
    low, high, low_t, high_t, spread = columns_of(run_t, k)
    causal = iota((LANES, LANES), 0) >= iota((LANES, LANES), 1)
    gaps = [jnp.where(causal, a - b, -1e30) for a, b in ((low_t, low), (high_t, high))]
    scaled = [jnp.exp(gap) * step_t[pl.ds(2 * k + i, 1), :] for i, gap in enumerate(gaps)]
    return jnp.concatenate(scaled, axis=0), spread


def projections(bc):
    lane = iota(bc.shape, 1)
    turned = pltpu.roll(bc.astype(F32), HEADDIM, 1)
    b_low = jnp.where(lane < DSTATE, bc.astype(F32), 0.0).astype(BF16)
    c_low = jnp.where(lane < DSTATE, turned, 0.0).astype(BF16)
    b_high = jnp.where(lane >= DSTATE, turned, 0.0).astype(BF16)
    return b_low, c_low, b_high


def head_sum(value, k):
    pick = (iota((LANES, LANES), 1) == 2 * k + iota((LANES, LANES), 0) // HEADDIM).astype(BF16)
    high = value.astype(BF16)
    return dot(high, pick) + dot((value - high.astype(F32)).astype(BF16), pick)


def state_tile(ref, k):
    return ref[pl.ds(4 * k, 4)].reshape(DSTATE, LANES)


def forward_kernel(x_ref, halo_ref, dt_ref, alog_ref, w_ref, mix_ref, end_ref, total_ref, lanes_ref, run_t, step_t):
    tiles = x_ref.shape[1] // LANES - 1
    _, _, running = steps_of(dt_ref, alog_ref, run_t, step_t)
    total_ref[...] = jnp.broadcast_to(running[-1:], total_ref.shape)
    lanes_ref[...] = jnp.zeros_like(lanes_ref)

    def mixin(k):
        at = tile_at(k)
        _, pre = conv_pre(x_ref[:, at].astype(F32), halo_ref[:, at], w_ref[:, at])
        mixed = (pre * sigmoid(pre)).astype(BF16)
        mix_ref[:, at] = mixed
        return mixed

    bc = mixin(tiles)

    def body(k, carry):
        mixed = mixin(k)
        spread = columns_of(run_t, k)[-1]
        to_end = jnp.exp(spread[-1:] - spread) * columns_of(step_t, k)[-1]
        lanes_ref[pl.ds(k, 1), :] = spread[-1:]
        ended = dot(bc, (mixed.astype(F32) * to_end).astype(BF16), 0, 0)
        end_ref[pl.ds(4 * k, 4)] = ended[:DSTATE].reshape(4, 16, LANES).astype(BF16)
        return carry

    lax.fori_loop(0, tiles, body, 0)
    spare = end_ref.shape[0] - 4 * tiles
    if spare:
        end_ref[4 * tiles :] = jnp.zeros((spare, 16, LANES), BF16)


def middle_kernel(
    mix_ref, z_ref, dt_ref, alog_ref, gain_ref, out_ref, start_ref,
    normed_ref, gz_ref, gmix_ref, gstart_ref, gain_part_ref, along_ref, gc_ref,
    run_t, step_t, mixer, sums,
):
    inner = z_ref.shape[1]
    tiles = inner // LANES
    steps_of(dt_ref, alog_ref, run_t, step_t)
    bc = mix_ref[:, inner : inner + LANES]
    b_low, c_low, _ = projections(bc)
    scores = dot(c_low, b_low, 1, 1)
    scores2 = jnp.concatenate([scores, scores], axis=0)
    lane = iota((LANES, LANES), 1)
    c_both = jnp.where(lane < DSTATE, c_low.astype(F32), bc.astype(F32)).astype(BF16)

    def parts_of(k):
        start = state_tile(start_ref, k)
        high = start.astype(BF16)
        return jnp.concatenate([(start - high.astype(F32)).astype(BF16), high], axis=0)

    sums[...] = jnp.zeros_like(sums)

    def first(k, carry):
        at = tile_at(k)
        scaled, spread = pair_weights(run_t, step_t, k)
        both = dot((scores2 * scaled).astype(BF16), mix_ref[:, at])
        within = jnp.where(lane < HEADDIM, both[:LANES], both[LANES:])
        carried = dot(c_both, parts_of(k))
        mixed = within + carried * jnp.exp(spread)
        mixer[:, at] = mixed
        z = z_ref[:, at].astype(F32)
        gated = mixed * z * sigmoid(z)
        sums[0] += gated * gated
        sums[1] += gated * out_ref[:, at].astype(F32) * gain_ref[0:1, at]
        return carry

    lax.fori_loop(0, tiles, first, 0)
    scale = lax.rsqrt(jnp.sum(sums[0], axis=1, keepdims=True) / inner + 1e-05)
    back = scale * scale * scale * (jnp.sum(sums[1], axis=1, keepdims=True) / inner)
    along_ref[...] = jnp.zeros_like(along_ref)
    gc_ref[...] = jnp.zeros_like(gc_ref)

    def second(k, carry):
        at = tile_at(k)
        spread = columns_of(run_t, k)[-1]
        mixed = mixer[:, at]
        z = z_ref[:, at].astype(F32)
        gate = sigmoid(z)
        gated = mixed * z * gate
        gain = gain_ref[0:1, at]
        out = out_ref[:, at].astype(F32)
        plain = gated * scale
        normed_ref[:, at] = (plain * gain).astype(BF16)
        gain_row = jnp.sum(out * plain, axis=0, keepdims=True)
        gain_part_ref[k] = jnp.broadcast_to(gain_row, (8, LANES))
        ggated = out * gain * scale - gated * back
        gz_ref[:, at] = (ggated * mixed * gate * (1.0 + z * (1.0 - gate))).astype(BF16)
        exact = ggated * z * gate
        gmixer = exact.astype(BF16)
        gmix_ref[:, at] = exact
        wide = gmixer.astype(F32)
        along_ref[...] += head_sum(wide * mixed, k)
        decayed = exact * jnp.exp(spread)
        high = decayed.astype(BF16)
        low = (decayed - high.astype(F32)).astype(BF16)
        placed = parts_of(k)
        gc_ref[...] += dot(high, placed, 1, 1) + dot(low, placed, 1, 1)
        started = dot(bc, high, 0, 0)
        gstart_ref[pl.ds(4 * k, 4)] = started[DSTATE:].reshape(4, 16, LANES).astype(BF16)
        return carry

    lax.fori_loop(0, tiles, second, 0)
    halves = gc_ref[...]
    gc_ref[...] = jnp.where(lane < DSTATE, 0.0, halves + pltpu.roll(halves, DSTATE, 1))
    spare = gstart_ref.shape[0] - 4 * tiles
    if spare:
        gstart_ref[4 * tiles :] = jnp.zeros((spare, 16, LANES), BF16)


def backward_kernel(
    x_ref, halo_ref, mix_ref, dt_ref, alog_ref, w_ref, gmix_ref, start_ref, gend_ref, gain_part_ref, along_ref, gc_ref,
    gx_ref, head_ref, tail_ref, gdt_ref, part_ref,
    run_t, step_t, gscores, gbc, into, after, carry_rows,
):
    inner = gmix_ref.shape[1]
    tiles = inner // LANES
    step, log_decay, _ = steps_of(dt_ref, alog_ref, run_t, step_t)
    bc = mix_ref[:, inner : inner + LANES]
    b_low, c_low, b_high = projections(bc)
    scores = dot(c_low, b_low, 1, 1)
    scores2 = jnp.concatenate([scores, scores], axis=0)
    lane = iota((LANES, LANES), 1)
    blank = jnp.zeros((DSTATE, LANES), BF16)
    for ref in (gscores, into, after, carry_rows):
        ref[...] = jnp.zeros_like(ref)
    gbc[...] = gc_ref[...]

    def conv_back(k, gmixin):
        at = tile_at(k)
        taps = w_ref[:, at]
        ext, pre = conv_pre(x_ref[:, at].astype(F32), halo_ref[:, at], taps)
        gate = sigmoid(pre)
        gpre = gmixin.astype(BF16).astype(F32) * gate * (1.0 + pre * (1.0 - gate))
        rows = gpre.shape[0]
        none = jnp.zeros((8, LANES), F32)
        padded = jnp.concatenate([none, gpre, none], axis=0)
        gext = sum(taps[o : o + 1] * padded[8 - o : 8 - o + rows + 8] for o in range(4))
        own = gext[3 : 3 + rows]
        gx_ref[:, at] = own.astype(BF16)
        tail_ref[:, at] = own[rows - 16 :]
        head_ref[:, at] = gext[:8]
        return [jnp.sum(gpre * ext[5 + o : 5 + o + rows], axis=0, keepdims=True) for o in range(4)]

    def body(k, carry):
        at = tile_at(k)
        values = mix_ref[:, at]
        gmixer = gmix_ref[:, at]
        scaled, spread = pair_weights(run_t, step_t, k)
        weights = (scores2 * scaled).astype(BF16)
        wide = jnp.concatenate([jnp.where(lane < HEADDIM, gmixer, 0.0), jnp.where(lane < HEADDIM, 0.0, gmixer)], axis=0)
        split = wide.astype(BF16)
        rest = (wide - split.astype(F32)).astype(BF16)
        gweights = (dot(split, values, 1, 1) + dot(rest, values, 1, 1)) * scaled
        gscores[...] += gweights[:LANES] + gweights[LANES:]
        gvalues = dot(weights, split, 0, 0)
        to_end = jnp.exp(spread[-1:] - spread) * columns_of(step_t, k)[-1]
        start, gend = state_tile(start_ref, k), state_tile(gend_ref, k)
        gend_low = jnp.concatenate([gend, blank], axis=0)
        gended = to_end * dot(bc, gend_low)
        values32 = values.astype(F32)
        into[...] += head_sum(values32 * gvalues, k)
        after[...] += head_sum(values32 * gended, k)
        moved = jnp.sum(start * gend.astype(F32), axis=0, keepdims=True) * jnp.exp(spread[-1:])
        carry_rows[...] += head_sum(jnp.broadcast_to(moved, (16, LANES)), k)
        gbc[...] += dot((values32 * to_end).astype(BF16), gend_low, 1, 1)
        taps = conv_back(k, gvalues + gended)
        part_ref[k] = jnp.concatenate(taps + [gain_part_ref[k][:1], jnp.zeros((3, LANES), F32)], axis=0)
        return carry

    lax.fori_loop(0, tiles, body, 0)
    gscore = gscores[...].astype(BF16)
    rest = (gscores[...] - gscore.astype(F32)).astype(BF16)
    from_scores = dot(gscore, c_low, 0, 0) + dot(gscore, b_high) + dot(rest, c_low, 0, 0) + dot(rest, b_high)
    taps = conv_back(tiles, gbc[...] + from_scores)
    rows = step.shape[0]
    later = (iota((rows, rows), 0) <= iota((rows, rows), 1)).astype(F32)
    earlier = (iota((rows, rows), 0) > iota((rows, rows), 1)).astype(F32)
    glog = dot_exact(later, along_ref[...] - into[...]) + dot_exact(earlier, after[...]) + carry_rows[0:1]
    gstep = (into[...] + after[...]) / step - jnp.exp(alog_ref[0:1]) * glog
    gdt_ref[...] = gstep * sigmoid(dt_ref[...])
    galog = jnp.sum(glog * log_decay, axis=0, keepdims=True)
    part_ref[tiles] = jnp.concatenate(taps + [galog, jnp.zeros((3, LANES), F32)], axis=0)
    spare = part_ref.shape[0] - tiles - 1
    if spare:
        part_ref[tiles + 1 :] = jnp.zeros((spare, 8, LANES), F32)


def greet_all(axis, n):
    me = lax.axis_index(axis)
    barrier = pltpu.get_barrier_semaphore()

    def greet(d, carry):
        pl.semaphore_signal(barrier, inc=1, device_id={axis: lax.rem(me + d, n)}, device_id_type=MESH)
        return carry

    lax.fori_loop(1, n, greet, 0)
    pl.semaphore_wait(barrier, n - 1)
    return me


def to_peer(src, dst, send_sem, recv_sem, axis, peer):
    return pltpu.make_async_remote_copy(
        src_ref=src, dst_ref=dst, send_sem=send_sem, recv_sem=recv_sem,
        device_id={axis: peer}, device_id_type=MESH,
    )


def over_peers(n, action):
    def one(d, carry):
        action(d)
        return carry

    lax.fori_loop(1, n, one, 0)


def exchange_kernel(
    n, axis, reverse, in_ref, lanes_ref, total_ref, out_ref, totals_ref, lanes_near,
    near, joined, held, decays, back, ret, passed, sems,
):
    chips = n // 2
    me = lax.axis_index(axis)
    chip, core = lax.div(me, 2), lax.rem(me, 2)
    sibling = me + 1 - 2 * core
    half = in_ref.shape[0] // 2
    per = half // chips

    def peer(d):
        return 2 * lax.rem(chip + d + chips, chips) + core

    barrier = pltpu.get_barrier_semaphore()
    pl.semaphore_signal(barrier, inc=1, device_id={axis: sibling}, device_id_type=MESH)
    over_peers(chips, lambda d: pl.semaphore_signal(barrier, inc=1, device_id={axis: peer(d)}, device_id_type=MESH))
    pl.semaphore_wait(barrier, chips)

    def block(j):
        return pl.ds(j * per, per)

    mine = core * half
    first = core == (1 if reverse else 0)
    swaps = [to_peer(in_ref.at[pl.ds((1 - core) * half, half)], near, sems.at[0, 0], sems.at[1, 0], axis, sibling)]
    if not reverse:
        swaps.append(to_peer(lanes_ref, lanes_near, sems.at[2, 0], sems.at[3, 0], axis, sibling))
        swaps.append(to_peer(total_ref, totals_ref.at[chips], sems.at[4, 0], sems.at[5, 0], axis, sibling))
    for swap in swaps:
        swap.start()
    for swap in swaps:
        swap.wait()

    def lane_decays(r):
        row = pl.ds(lax.div(mine, 4) + r, 1)
        return jnp.exp(lanes_ref[row, :]), jnp.exp(lanes_near[row, :])

    def join(r, carry):
        own, other = lane_decays(r)
        at = pl.ds(4 * r, 4)
        own_state = in_ref[pl.ds(mine + 4 * r, 4)].astype(F32)
        other_state = near[at].astype(F32)
        summed = own_state * jnp.where(first, other, 1.0) + other_state * jnp.where(first, 1.0, own)
        joined[at] = summed.astype(BF16)
        return carry

    lax.fori_loop(0, half // 4, join, 0)

    def outgoing(d):
        there = lax.rem(chip + d, chips)
        return to_peer(joined.at[block(there)], held.at[d], sems.at[0, d], sems.at[1, d], axis, peer(d))

    def totals_out(d):
        return to_peer(totals_ref.at[0], totals_ref.at[d], sems.at[2, d], sems.at[3, d], axis, peer(d))

    if not reverse:
        totals_ref[0] = total_ref[...] + totals_ref[chips]
        over_peers(chips, lambda d: totals_out(d).start())
    over_peers(chips, lambda d: outgoing(d).start())
    held[0] = joined[block(chip)]
    if not reverse:
        over_peers(chips, lambda d: totals_out(d).wait())
    logs = totals_ref[:chips].reshape(chips * 8, LANES)
    for i in range(per):
        pair = lax.div(mine + chip * per + i, 4)
        pick = iota((LANES, LANES), 0) == 2 * pair + iota((LANES, LANES), 1) // HEADDIM
        decays[:, i] = jnp.exp(dot_exact(logs, pick.astype(F32))).reshape(chips, 8, LANES)
    over_peers(chips, lambda d: outgoing(d).wait())

    def advance(step, state):
        j = chips - 1 - step if reverse else step
        d = lax.rem(chip - j + chips, chips)
        back[lax.rem(j - chip + chips, chips)] = state.astype(back.dtype)
        return decays[d][:, :1] * state + held[d].astype(F32)

    lax.fori_loop(0, chips, advance, jnp.zeros((per, 16, LANES), F32))

    def returning(d):
        return to_peer(back.at[d], ret.at[block(chip)], sems.at[4, d], sems.at[5, d], axis, peer(d))

    def arriving(d):
        there = lax.rem(chip - d + chips, chips)
        return to_peer(back.at[d], ret.at[block(there)], sems.at[4, d], sems.at[5, d], axis, peer(-d))

    over_peers(chips, lambda d: returning(d).start())
    ret[block(chip)] = back[0]
    over_peers(chips, lambda d: returning(d).wait_send())
    over_peers(chips, lambda d: arriving(d).wait_recv())

    def hand(r, carry):
        own, other = lane_decays(r)
        at = pl.ds(4 * r, 4)
        own_state = in_ref[pl.ds(mine + 4 * r, 4)].astype(F32)
        other_state = near[at].astype(F32)
        begun = ret[at].astype(F32)
        moved = jnp.where(first, own, other) * begun + jnp.where(first, own_state, other_state)
        out_ref[pl.ds(mine + 4 * r, 4)] = jnp.where(first, begun, moved).astype(out_ref.dtype)
        passed[at] = jnp.where(first, moved, begun).astype(passed.dtype)
        return carry

    lax.fori_loop(0, half // 4, hand, 0)
    final = to_peer(passed, out_ref.at[pl.ds(mine, half)], sems.at[6, 0], sems.at[7, 0], axis, sibling)
    final.start()
    final.wait_send()
    to_peer(passed, out_ref.at[pl.ds((1 - core) * half, half)], sems.at[6, 0], sems.at[7, 0], axis, sibling).wait_recv()


def total_kernel(n, axis, part_ref, head_ref, out_ref, rows_ref, held, sems):
    me = greet_all(axis, n)
    per = part_ref.shape[0] // n

    def block(j):
        return pl.ds(j * per, per)

    def outgoing(d):
        return to_peer(part_ref.at[block(lax.rem(me + d, n))], held.at[d], sems.at[0, d], sems.at[1, d], axis, lax.rem(me + d, n))

    over_peers(n, lambda d: outgoing(d).start())
    rim = to_peer(head_ref, rows_ref, sems.at[2, 0], sems.at[3, 0], axis, lax.rem(me + n - 1, n))
    rim.start()
    held[0] = part_ref[block(me)]
    over_peers(n, lambda d: outgoing(d).wait())

    def add(d, total):
        return total + held[d]

    held[0] = lax.fori_loop(1, n, add, held[0])
    out_ref[block(me)] = held[0]

    def returning(d):
        return to_peer(held.at[0], out_ref.at[block(me)], sems.at[2, d], sems.at[3, d], axis, lax.rem(me + d, n))

    def arriving(d):
        source = lax.rem(me - d + n, n)
        return to_peer(held.at[0], out_ref.at[block(source)], sems.at[2, d], sems.at[3, d], axis, source)

    over_peers(n, lambda d: returning(d).start())
    over_peers(n, lambda d: returning(d).wait_send())
    over_peers(n, lambda d: arriving(d).wait_recv())
    rim.wait()


def call(kernel, operands, outs, scratch, **params):
    whole = pl.BlockSpec(memory_space=pltpu.VMEM)
    return pl.pallas_call(
        kernel,
        out_shape=[jax.ShapeDtypeStruct(shape, dtype) for shape, dtype in outs],
        in_specs=[whole] * len(operands),
        out_specs=[whole] * len(outs),
        scratch_shapes=scratch,
        compiler_params=pltpu.CompilerParams(vmem_limit_bytes=VMEM_LIMIT, **params),
    )(*operands)


def exchange(axis, n, reverse, tiles, lanes, totals, lanes_near=None):
    chips, half = n // 2, tiles.shape[0] // 2
    per = half // chips
    kept = BF16 if reverse else F32
    near, joined, ret, passed = [pltpu.VMEM((half, 16, LANES), held_as) for held_as in (BF16, BF16, kept, kept)]
    slots, back = [pltpu.VMEM((chips, per, 16, LANES), held_as) for held_as in (BF16, kept)]
    scratch = [
        near, joined, slots, pltpu.VMEM((chips, per, 8, LANES), F32), back, ret, passed,
        pltpu.SemaphoreType.DMA((8, chips)),
    ]
    outs = [(tiles.shape, kept)]
    operands = [tiles, lanes, totals]
    if reverse:
        operands.append(lanes_near)

        def kernel(in_ref, lanes_ref, totals_ref, near_ref, out_ref, *rest):
            exchange_kernel(n, axis, True, in_ref, lanes_ref, None, out_ref, totals_ref, near_ref, *rest)
    else:
        kernel = functools.partial(exchange_kernel, n, axis, False)
        outs += [((chips + 1, 8, LANES), F32), (lanes.shape, F32)]
    return call(kernel, operands, outs, scratch, collective_id=1 + reverse, has_side_effects=True)


def on_device(xbc_raw, gate_z, dt_raw, a_log, conv_weight, norm_gain, grad_out):
    axis = "context"
    n = lax.axis_size(axis)
    rows, inner = gate_z.shape
    channels = xbc_raw.shape[1]
    heads = a_log.shape[0]
    tiles = inner // LANES
    unit = n * 8 // math.gcd(n, 8)
    state_tiles = -(-4 * tiles // unit) * unit
    lane_rows = -(-state_tiles // 32) * 8
    part_tiles = -(-(tiles + 1) // n) * n
    rim = lax.ppermute(xbc_raw[rows - 3 :], axis, [(i, i + 1) for i in range(n - 1)])
    halo = jnp.pad(rim.astype(F32), ((5, 0), (0, 0)))
    dt = jnp.pad(dt_raw, ((0, 0), (0, LANES - heads)))
    alog = jnp.pad(a_log, (0, LANES - heads))[None]
    per_head = [pltpu.VMEM((LANES, rows), F32)] * 2
    square = pltpu.VMEM((rows, LANES), F32)

    mixin, ended, total, lanes = call(
        forward_kernel, (xbc_raw, halo, dt, alog, conv_weight),
        [((rows, channels), BF16), ((state_tiles, 16, LANES), BF16), ((8, LANES), F32), ((lane_rows, LANES), F32)], per_head,
    )
    start, totals, lanes_near = exchange(axis, n, False, ended, lanes, total)
    normed, grad_z, gmixer, gstart, gain_part, along, gc = call(
        middle_kernel, (mixin, gate_z, dt, alog, norm_gain[None], grad_out, start),
        [
            ((rows, inner), BF16), ((rows, inner), BF16), ((rows, inner), F32),
            ((state_tiles, 16, LANES), BF16), ((tiles, 8, LANES), F32), ((rows, LANES), F32),
            ((rows, LANES), F32),
        ],
        per_head + [pltpu.VMEM((rows, inner), F32), pltpu.VMEM((2, rows, LANES), F32)],
    )
    (gend,) = exchange(axis, n, True, gstart, lanes, totals, lanes_near)
    gx, head, tail, gdt, part = call(
        backward_kernel,
        (xbc_raw, halo, mixin, dt, alog, conv_weight, gmixer, start, gend, gain_part, along, gc),
        [
            ((rows, channels), BF16), ((8, channels), F32), ((16, channels), F32),
            ((rows, LANES), F32), ((part_tiles, 8, LANES), F32),
        ],
        per_head + [square] * 4 + [pltpu.VMEM((16, LANES), F32)],
    )
    sums, back_rows = call(
        functools.partial(total_kernel, n, axis), (part, head),
        [((part_tiles, 8, LANES), F32), ((8, channels), F32)],
        [pltpu.VMEM((n, part_tiles // n, 8, LANES), F32), pltpu.SemaphoreType.DMA((4, n))],
        collective_id=3, has_side_effects=True,
    )
    borrowed = jnp.where(lax.axis_index(axis) < n - 1, back_rows[:3], 0.0)
    fixed = (tail + jnp.pad(borrowed, ((13, 0), (0, 0)))).astype(BF16)
    grad_xbc = lax.dynamic_update_slice(gx, fixed, (rows - 16, 0))
    conv_total = sums[: tiles + 1, :4].transpose(1, 0, 2).reshape(4, channels)
    return (
        normed, grad_xbc, grad_z, gdt[:, :heads], conv_total,
        sums[tiles, 4, :heads], sums[:tiles, 4].reshape(inner),
    )


def solution(mesh):
    split = P(("groups", "context"), None)
    return jax.shard_map(
        on_device,
        mesh=mesh,
        in_specs=(split, split, split, P(), P(), P(), split),
        out_specs=(split, split, split, split, P("groups", None), P("groups"), P("groups")),
        check_vma=False,
    )
```

```python
import functools
import math

import jax
import jax.numpy as jnp
from jax import lax
from jax.experimental import pallas as pl
from jax.experimental.pallas import tpu as pltpu
from jax.sharding import PartitionSpec as P

HEADDIM = 64
DSTATE = 64
LANES = 128
MESH = pl.DeviceIdType.MESH
F32 = jnp.float32
BF16 = jnp.bfloat16
VMEM_LIMIT = 48 * 1024 * 1024


def dot(a, b, ca=1, cb=0):
    return lax.dot_general(a, b, (((ca,), (cb,)), ((), ())), preferred_element_type=F32)


def dot_exact(a, b):
    return jnp.dot(a, b, precision=lax.Precision.HIGHEST, preferred_element_type=F32)


def iota(shape, axis):
    return lax.broadcasted_iota(jnp.int32, shape, axis)


def tile_at(k):
    return pl.ds(pl.multiple_of(k * LANES, LANES), LANES)


def conv_pre(x, halo, taps):
    ext = jnp.concatenate([halo, x], axis=0)
    rows = x.shape[0]
    return ext, sum(taps[o : o + 1] * ext[5 + o : 5 + o + rows] for o in range(4))


def sigmoid(v):
    return 1.0 / (1.0 + jnp.exp(-v))


def steps_of(dt_ref, alog_ref, run_t, step_t):
    raw = dt_ref[...]
    step = jnp.maximum(raw, 0.0) + jnp.log1p(jnp.exp(-jnp.abs(raw)))
    log_decay = -jnp.exp(alog_ref[0:1]) * step
    rows = raw.shape[0]
    tri = (iota((rows, rows), 0) >= iota((rows, rows), 1)).astype(F32)
    running = dot_exact(tri, log_decay)
    run_t[...] = running.T
    step_t[...] = step.T
    return step, log_decay, running


def columns_of(row_ref, k):
    low = jnp.broadcast_to(row_ref[pl.ds(2 * k, 1), :], (LANES, LANES))
    high = jnp.broadcast_to(row_ref[pl.ds(2 * k + 1, 1), :], (LANES, LANES))
    low_t, high_t = low.T, high.T
    return low, high, low_t, high_t, jnp.where(iota((LANES, LANES), 1) < HEADDIM, low_t, high_t)


def pair_weights(run_t, step_t, k):
    low, high, low_t, high_t, spread = columns_of(run_t, k)
    causal = iota((LANES, LANES), 0) >= iota((LANES, LANES), 1)
    gaps = [jnp.where(causal, a - b, -1e30) for a, b in ((low_t, low), (high_t, high))]
    scaled = [jnp.exp(gap) * step_t[pl.ds(2 * k + i, 1), :] for i, gap in enumerate(gaps)]
    return jnp.concatenate(scaled, axis=0), spread


def projections(bc):
    lane = iota(bc.shape, 1)
    turned = pltpu.roll(bc.astype(F32), HEADDIM, 1)
    b_low = jnp.where(lane < DSTATE, bc.astype(F32), 0.0).astype(BF16)
    c_low = jnp.where(lane < DSTATE, turned, 0.0).astype(BF16)
    b_high = jnp.where(lane >= DSTATE, turned, 0.0).astype(BF16)
    return b_low, c_low, b_high


def head_sum(value, k):
    pick = (iota((LANES, LANES), 1) == 2 * k + iota((LANES, LANES), 0) // HEADDIM).astype(BF16)
    high = value.astype(BF16)
    return dot(high, pick) + dot((value - high.astype(F32)).astype(BF16), pick)


def state_tile(ref, k):
    return ref[pl.ds(4 * k, 4)].reshape(DSTATE, LANES)


def forward_part(x_ref, halo_ref, w_ref, run_t, step_t, mix_ref, end_ref, lanes_ref):
    tiles = x_ref.shape[1] // LANES - 1
    lanes_ref[...] = jnp.zeros_like(lanes_ref)

    def mixin(k):
        at = tile_at(k)
        _, pre = conv_pre(x_ref[:, at].astype(F32), halo_ref[:, at], w_ref[:, at])
        mixed = (pre * sigmoid(pre)).astype(BF16)
        mix_ref[:, at] = mixed
        return mixed

    bc = mixin(tiles)

    def body(k, carry):
        mixed = mixin(k)
        spread = columns_of(run_t, k)[-1]
        to_end = jnp.exp(spread[-1:] - spread) * columns_of(step_t, k)[-1]
        lanes_ref[pl.ds(k, 1), :] = spread[-1:]
        ended = dot(bc, (mixed.astype(F32) * to_end).astype(BF16), 0, 0)
        end_ref[pl.ds(4 * k, 4)] = ended[:DSTATE].reshape(4, 16, LANES).astype(BF16)
        return carry

    lax.fori_loop(0, tiles, body, 0, unroll=2)
    spare = end_ref.shape[0] - 4 * tiles
    if spare:
        end_ref[4 * tiles :] = jnp.zeros((spare, 16, LANES), BF16)


def scores_of(bc):
    b_low, c_low, b_high = projections(bc)
    scores = dot(c_low, b_low, 1, 1)
    return b_low, c_low, b_high, jnp.concatenate([scores, scores], axis=0)


def within_part(begin, end, mix_ref, scores2, run_t, step_t, mixer):
    lane = iota((LANES, LANES), 1)

    def body(k, carry):
        at = tile_at(k)
        scaled, _ = pair_weights(run_t, step_t, k)
        both = dot((scores2[...] * scaled).astype(BF16), mix_ref[:, at])
        mixer[:, at] = jnp.where(lane < HEADDIM, both[:LANES], both[LANES:])
        return carry

    lax.fori_loop(begin, end, body, 0, unroll=2)


def middle_part(
    mix_ref, z_ref, gain_ref, out_ref, start_ref, run_t, mixer,
    normed_ref, gz_ref, gmix_ref, gstart_ref, gain_part_ref, along_ref, gc_ref, sums,
):
    inner = z_ref.shape[1]
    tiles = inner // LANES
    bc = mix_ref[:, inner : inner + LANES]
    _, c_low, _ = projections(bc)
    lane = iota((LANES, LANES), 1)
    c_both = jnp.where(lane < DSTATE, c_low.astype(F32), bc.astype(F32)).astype(BF16)

    def parts_of(k):
        start = state_tile(start_ref, k)
        high = start.astype(BF16)
        return jnp.concatenate([(start - high.astype(F32)).astype(BF16), high], axis=0)

    sums[...] = jnp.zeros_like(sums)

    def first(k, carry):
        at = tile_at(k)
        spread = columns_of(run_t, k)[-1]
        carried = dot(c_both, parts_of(k))
        mixed = mixer[:, at] + carried * jnp.exp(spread)
        mixer[:, at] = mixed
        z = z_ref[:, at].astype(F32)
        gated = mixed * z * sigmoid(z)
        sums[0] += gated * gated
        sums[1] += gated * out_ref[:, at].astype(F32) * gain_ref[0:1, at]
        return carry

    lax.fori_loop(0, tiles, first, 0, unroll=2)
    scale = lax.rsqrt(jnp.sum(sums[0], axis=1, keepdims=True) / inner + 1e-05)
    back = scale * scale * scale * (jnp.sum(sums[1], axis=1, keepdims=True) / inner)
    along_ref[...] = jnp.zeros_like(along_ref)
    gc_ref[...] = jnp.zeros_like(gc_ref)

    def second(k, carry):
        at = tile_at(k)
        spread = columns_of(run_t, k)[-1]
        mixed = mixer[:, at]
        z = z_ref[:, at].astype(F32)
        gate = sigmoid(z)
        gated = mixed * z * gate
        gain = gain_ref[0:1, at]
        out = out_ref[:, at].astype(F32)
        plain = gated * scale
        normed_ref[:, at] = (plain * gain).astype(BF16)
        gain_row = jnp.sum(out * plain, axis=0, keepdims=True)
        gain_part_ref[k] = jnp.broadcast_to(gain_row, (8, LANES))
        ggated = out * gain * scale - gated * back
        gz_ref[:, at] = (ggated * mixed * gate * (1.0 + z * (1.0 - gate))).astype(BF16)
        exact = ggated * z * gate
        gmixer = exact.astype(BF16)
        gmix_ref[:, at] = exact
        wide = gmixer.astype(F32)
        along_ref[...] += head_sum(wide * mixed, k)
        decayed = exact * jnp.exp(spread)
        high = decayed.astype(BF16)
        low = (decayed - high.astype(F32)).astype(BF16)
        placed = parts_of(k)
        gc_ref[...] += dot(high, placed, 1, 1) + dot(low, placed, 1, 1)
        started = dot(bc, high, 0, 0)
        gstart_ref[pl.ds(4 * k, 4)] = started[DSTATE:].reshape(4, 16, LANES).astype(BF16)
        return carry

    lax.fori_loop(0, tiles, second, 0, unroll=2)
    halves = gc_ref[...]
    gc_ref[...] = jnp.where(lane < DSTATE, 0.0, halves + pltpu.roll(halves, DSTATE, 1))
    spare = gstart_ref.shape[0] - 4 * tiles
    if spare:
        gstart_ref[4 * tiles :] = jnp.zeros((spare, 16, LANES), BF16)


def within_back(begin, end, mix_ref, gmix_ref, scores2, run_t, step_t, gscores, gval, into):
    lane = iota((LANES, LANES), 1)

    def body(k, carry):
        at = tile_at(k)
        values = mix_ref[:, at]
        gmixer = gmix_ref[:, at]
        scaled, _ = pair_weights(run_t, step_t, k)
        weights = (scores2[...] * scaled).astype(BF16)
        wide = jnp.concatenate([jnp.where(lane < HEADDIM, gmixer, 0.0), jnp.where(lane < HEADDIM, 0.0, gmixer)], axis=0)
        split = wide.astype(BF16)
        rest = (wide - split.astype(F32)).astype(BF16)
        gweights = (dot(split, values, 1, 1) + dot(rest, values, 1, 1)) * scaled
        gscores[...] += gweights[:LANES] + gweights[LANES:]
        gvalues = dot(weights, split, 0, 0)
        into[...] += head_sum(values.astype(F32) * gvalues, k)
        gval[:, at] = gvalues
        return carry

    lax.fori_loop(begin, end, body, 0, unroll=2)


def backward_part(
    x_ref, halo_ref, mix_ref, dt_ref, alog_ref, w_ref, start_ref, gend_ref, gain_part_ref, along_ref, gbc,
    step_ref, decay_ref, run_t, step_t, gscores, gval, into, after, carry_rows,
    gx_ref, head_ref, tail_ref, gdt_ref, part_ref,
):
    inner = gval.shape[1]
    tiles = inner // LANES
    bc = mix_ref[:, inner : inner + LANES]
    _, c_low, b_high = projections(bc)
    blank = jnp.zeros((DSTATE, LANES), BF16)
    after[...] = jnp.zeros_like(after)
    carry_rows[...] = jnp.zeros_like(carry_rows)

    def conv_back(k, gmixin):
        at = tile_at(k)
        taps = w_ref[:, at]
        ext, pre = conv_pre(x_ref[:, at].astype(F32), halo_ref[:, at], taps)
        gate = sigmoid(pre)
        gpre = gmixin.astype(BF16).astype(F32) * gate * (1.0 + pre * (1.0 - gate))
        rows = gpre.shape[0]
        none = jnp.zeros((8, LANES), F32)
        padded = jnp.concatenate([none, gpre, none], axis=0)
        gext = sum(taps[o : o + 1] * padded[8 - o : 8 - o + rows + 8] for o in range(4))
        own = gext[3 : 3 + rows]
        gx_ref[:, at] = own.astype(BF16)
        tail_ref[:, at] = own[rows - 16 :]
        head_ref[:, at] = gext[:8]
        return [jnp.sum(gpre * ext[5 + o : 5 + o + rows], axis=0, keepdims=True) for o in range(4)]

    def body(k, carry):
        values = mix_ref[:, tile_at(k)]
        spread = columns_of(run_t, k)[-1]
        to_end = jnp.exp(spread[-1:] - spread) * columns_of(step_t, k)[-1]
        start, gend = state_tile(start_ref, k), state_tile(gend_ref, k)
        gend_low = jnp.concatenate([gend, blank], axis=0)
        gended = to_end * dot(bc, gend_low)
        values32 = values.astype(F32)
        after[...] += head_sum(values32 * gended, k)
        moved = jnp.sum(start * gend.astype(F32), axis=0, keepdims=True) * jnp.exp(spread[-1:])
        carry_rows[...] += head_sum(jnp.broadcast_to(moved, (16, LANES)), k)
        gbc[...] += dot((values32 * to_end).astype(BF16), gend_low, 1, 1)
        taps = conv_back(k, gval[:, tile_at(k)] + gended)
        part_ref[k] = jnp.concatenate(taps + [gain_part_ref[k][:1], jnp.zeros((3, LANES), F32)], axis=0)
        return carry

    lax.fori_loop(0, tiles, body, 0, unroll=2)
    gscore = gscores[...].astype(BF16)
    rest = (gscores[...] - gscore.astype(F32)).astype(BF16)
    from_scores = dot(gscore, c_low, 0, 0) + dot(gscore, b_high) + dot(rest, c_low, 0, 0) + dot(rest, b_high)
    taps = conv_back(tiles, gbc[...] + from_scores)
    step, log_decay = step_ref[...], decay_ref[...]
    rows = step.shape[0]
    later = (iota((rows, rows), 0) <= iota((rows, rows), 1)).astype(F32)
    earlier = (iota((rows, rows), 0) > iota((rows, rows), 1)).astype(F32)
    glog = dot_exact(later, along_ref[...] - into[...]) + dot_exact(earlier, after[...]) + carry_rows[0:1]
    gstep = (into[...] + after[...]) / step - jnp.exp(alog_ref[0:1]) * glog
    gdt_ref[...] = gstep * sigmoid(dt_ref[...])
    galog = jnp.sum(glog * log_decay, axis=0, keepdims=True)
    part_ref[tiles] = jnp.concatenate(taps + [galog, jnp.zeros((3, LANES), F32)], axis=0)
    spare = part_ref.shape[0] - tiles - 1
    if spare:
        part_ref[tiles + 1 :] = jnp.zeros((spare, 8, LANES), F32)


def greet_all(axis, n):
    me = lax.axis_index(axis)
    barrier = pltpu.get_barrier_semaphore()

    def greet(d, carry):
        pl.semaphore_signal(barrier, inc=1, device_id={axis: lax.rem(me + d, n)}, device_id_type=MESH)
        return carry

    lax.fori_loop(1, n, greet, 0)
    pl.semaphore_wait(barrier, n - 1)
    return me


def to_peer(src, dst, send_sem, recv_sem, axis, peer):
    return pltpu.make_async_remote_copy(
        src_ref=src, dst_ref=dst, send_sem=send_sem, recv_sem=recv_sem,
        device_id={axis: peer}, device_id_type=MESH,
    )


def over_peers(n, action):
    def one(d, carry):
        action(d)
        return carry

    lax.fori_loop(1, n, one, 0)


def exchange_part(
    n, axis, reverse, in_ref, lanes_ref, total_ref, out_ref, totals_ref, lanes_near,
    near, joined, held, decays, back, ret, passed, sems, meanwhile, finish,
):
    chips = n // 2
    me = lax.axis_index(axis)
    chip, core = lax.div(me, 2), lax.rem(me, 2)
    sibling = me + 1 - 2 * core
    half = in_ref.shape[0] // 2
    per = half // chips

    def peer(d):
        return 2 * lax.rem(chip + d + chips, chips) + core

    def block(j):
        return pl.ds(j * per, per)

    mine = core * half
    first = core == (1 if reverse else 0)
    swaps = [to_peer(in_ref.at[pl.ds((1 - core) * half, half)], near, sems.at[0, 0], sems.at[1, 0], axis, sibling)]
    if not reverse:
        swaps.append(to_peer(lanes_ref, lanes_near, sems.at[2, 0], sems.at[3, 0], axis, sibling))
        swaps.append(to_peer(total_ref, totals_ref.at[chips], sems.at[4, 0], sems.at[5, 0], axis, sibling))
    for swap in swaps:
        swap.start()
    for swap in swaps:
        swap.wait()

    def lane_decays(r):
        row = pl.ds(lax.div(mine, 4) + r, 1)
        return jnp.exp(lanes_ref[row, :]), jnp.exp(lanes_near[row, :])

    def join(r, carry):
        own, other = lane_decays(r)
        at = pl.ds(4 * r, 4)
        own_state = in_ref[pl.ds(mine + 4 * r, 4)].astype(F32)
        other_state = near[at].astype(F32)
        summed = own_state * jnp.where(first, other, 1.0) + other_state * jnp.where(first, 1.0, own)
        joined[at] = summed.astype(BF16)
        return carry

    lax.fori_loop(0, half // 4, join, 0)

    def outgoing(d):
        there = lax.rem(chip + d, chips)
        return to_peer(joined.at[block(there)], held.at[d], sems.at[0, d], sems.at[1, d], axis, peer(d))

    def totals_out(d):
        return to_peer(totals_ref.at[0], totals_ref.at[d], sems.at[2, d], sems.at[3, d], axis, peer(d))

    if not reverse:
        totals_ref[0] = total_ref[...] + totals_ref[chips]
        over_peers(chips, lambda d: totals_out(d).start())
    over_peers(chips, lambda d: outgoing(d).start())
    held[0] = joined[block(chip)]
    if not reverse:
        over_peers(chips, lambda d: totals_out(d).wait())
    logs = totals_ref[:chips].reshape(chips * 8, LANES)
    for i in range(per):
        pair = lax.div(mine + chip * per + i, 4)
        pick = iota((LANES, LANES), 0) == 2 * pair + iota((LANES, LANES), 1) // HEADDIM
        decays[:, i] = jnp.exp(dot_exact(logs, pick.astype(F32))).reshape(chips, 8, LANES)
    meanwhile()
    over_peers(chips, lambda d: outgoing(d).wait())

    def advance(step, state):
        j = chips - 1 - step if reverse else step
        d = lax.rem(chip - j + chips, chips)
        back[lax.rem(j - chip + chips, chips)] = state.astype(back.dtype)
        return decays[d][:, :1] * state + held[d].astype(F32)

    lax.fori_loop(0, chips, advance, jnp.zeros((per, 16, LANES), F32))

    def returning(d):
        return to_peer(back.at[d], ret.at[block(chip)], sems.at[4, d], sems.at[5, d], axis, peer(d))

    def arriving(d):
        there = lax.rem(chip - d + chips, chips)
        return to_peer(back.at[d], ret.at[block(there)], sems.at[4, d], sems.at[5, d], axis, peer(-d))

    over_peers(chips, lambda d: returning(d).start())
    ret[block(chip)] = back[0]
    finish()
    over_peers(chips, lambda d: returning(d).wait_send())
    over_peers(chips, lambda d: arriving(d).wait_recv())

    def hand(r, carry):
        own, other = lane_decays(r)
        at = pl.ds(4 * r, 4)
        own_state = in_ref[pl.ds(mine + 4 * r, 4)].astype(F32)
        other_state = near[at].astype(F32)
        begun = ret[at].astype(F32)
        moved = jnp.where(first, own, other) * begun + jnp.where(first, own_state, other_state)
        out_ref[pl.ds(mine + 4 * r, 4)] = jnp.where(first, begun, moved).astype(out_ref.dtype)
        passed[at] = jnp.where(first, moved, begun).astype(passed.dtype)
        return carry

    lax.fori_loop(0, half // 4, hand, 0)
    final = to_peer(passed, out_ref.at[pl.ds(mine, half)], sems.at[6, 0], sems.at[7, 0], axis, sibling)
    final.start()
    final.wait_send()
    to_peer(passed, out_ref.at[pl.ds((1 - core) * half, half)], sems.at[6, 0], sems.at[7, 0], axis, sibling).wait_recv()


def total_part(n, axis, part_ref, head_ref, out_ref, rows_ref, held, sems):
    me = lax.axis_index(axis)
    per = part_ref.shape[0] // n

    def block(j):
        return pl.ds(j * per, per)

    def outgoing(d):
        return to_peer(part_ref.at[block(lax.rem(me + d, n))], held.at[d], sems.at[0, d], sems.at[1, d], axis, lax.rem(me + d, n))

    over_peers(n, lambda d: outgoing(d).start())
    rim = to_peer(head_ref, rows_ref, sems.at[2, 0], sems.at[3, 0], axis, lax.rem(me + n - 1, n))
    rim.start()
    held[0] = part_ref[block(me)]
    over_peers(n, lambda d: outgoing(d).wait())

    def add(d, total):
        return total + held[d]

    held[0] = lax.fori_loop(1, n, add, held[0])
    out_ref[block(me)] = held[0]

    def returning(d):
        return to_peer(held.at[0], out_ref.at[block(me)], sems.at[2, d], sems.at[3, d], axis, lax.rem(me + d, n))

    def arriving(d):
        source = lax.rem(me - d + n, n)
        return to_peer(held.at[0], out_ref.at[block(source)], sems.at[2, d], sems.at[3, d], axis, source)

    over_peers(n, lambda d: returning(d).start())
    over_peers(n, lambda d: returning(d).wait_send())
    over_peers(n, lambda d: arriving(d).wait_recv())
    rim.wait()


def whole_kernel(
    n, axis,
    x_ref, z_ref, dt_ref, alog_ref, w_ref, gain_ref, out_ref,
    normed_ref, gx_ref, gz_ref, gdt_ref, sums_ref,
    rim, halo, run_t, step_t, step_ref, decay_ref, mix, scores2, mixer, gmix, gval,
    ended, gstart, start, gend, lanes, lanes_near, total, totals,
    gain_part, along, gc, norm_sums, gscores, into, after, carry_rows,
    part, head, tail, back_rows, total_held, rim_sems, total_sems, *states,
):
    rows, inner = z_ref.shape
    tiles = inner // LANES
    middle = tiles // 4 * 2
    me = greet_all(axis, n)
    last = to_peer(x_ref.at[rows - 16 :], rim, rim_sems.at[0], rim_sems.at[1], axis, lax.rem(me + 1, n))
    last.start()
    step, log_decay, running = steps_of(dt_ref, alog_ref, run_t, step_t)
    step_ref[...] = step
    decay_ref[...] = log_decay
    total[...] = jnp.broadcast_to(running[-1:], total.shape)
    last.wait()
    halo[...] = jnp.where(me > 0, rim[...].astype(F32)[8:], 0.0)
    forward_part(x_ref, halo, w_ref, run_t, step_t, mix, ended, lanes)
    scores2[...] = scores_of(mix[:, inner : inner + LANES])[3]

    def within(begin, end):
        return lambda: within_part(begin, end, mix, scores2, run_t, step_t, mixer)

    exchange_part(
        n, axis, False, ended, lanes, total, start, totals, lanes_near, *states[:8],
        within(0, middle), within(middle, tiles),
    )
    middle_part(
        mix, z_ref, gain_ref, out_ref, start, run_t, mixer,
        normed_ref, gz_ref, gmix, gstart, gain_part, along, gc, norm_sums,
    )
    gscores[...] = jnp.zeros_like(gscores)
    into[...] = jnp.zeros_like(into)

    def back(begin, end):
        return lambda: within_back(begin, end, mix, gmix, scores2, run_t, step_t, gscores, gval, into)

    exchange_part(
        n, axis, True, gstart, lanes, None, gend, totals, lanes_near, *states[8:],
        back(0, middle), back(middle, tiles),
    )
    backward_part(
        x_ref, halo, mix, dt_ref, alog_ref, w_ref, start, gend, gain_part, along, gc,
        step_ref, decay_ref, run_t, step_t, gscores, gval, into, after, carry_rows,
        gx_ref, head, tail, gdt_ref, part,
    )
    total_part(n, axis, part, head, sums_ref, back_rows, total_held, total_sems)

    def mend(k, carry):
        at = tile_at(k)
        borrowed = jnp.where((iota((8, LANES), 0) < 3) & (me < n - 1), back_rows[:, at], 0.0)
        moved = jnp.concatenate([jnp.zeros((8, LANES), F32), pltpu.roll(borrowed, 5, 0)], axis=0)
        gx_ref[rows - 16 :, at] = (tail[:, at] + moved).astype(BF16)
        return carry

    lax.fori_loop(0, tiles + 1, mend, 0)


def on_device(xbc_raw, gate_z, dt_raw, a_log, conv_weight, norm_gain, grad_out):
    axis = "context"
    n = lax.axis_size(axis)
    rows, inner = gate_z.shape
    channels = xbc_raw.shape[1]
    heads = a_log.shape[0]
    tiles = inner // LANES
    unit = n * 8 // math.gcd(n, 8)
    state_tiles = -(-4 * tiles // unit) * unit
    lane_rows = -(-state_tiles // 32) * 8
    part_tiles = -(-(tiles + 1) // n) * n
    dt = jnp.pad(dt_raw, ((0, 0), (0, LANES - heads)))
    alog = jnp.pad(a_log, (0, LANES - heads))[None]
    chips, half = n // 2, state_tiles // 2
    per = half // chips
    vmem = pltpu.VMEM
    square = vmem((rows, LANES), F32)
    wide = vmem((rows, inner), F32)

    def states(kept):
        return [
            vmem((half, 16, LANES), BF16), vmem((half, 16, LANES), BF16), vmem((chips, per, 16, LANES), BF16),
            vmem((chips, per, 8, LANES), F32), vmem((chips, per, 16, LANES), kept),
            vmem((half, 16, LANES), kept), vmem((half, 16, LANES), kept), pltpu.SemaphoreType.DMA((8, chips)),
        ]

    scratch = [
        vmem((16, channels), BF16), vmem((8, channels), F32), vmem((LANES, rows), F32), vmem((LANES, rows), F32),
        square, square, vmem((rows, channels), BF16), vmem((2 * rows, LANES), F32), wide, wide, wide,
        vmem((state_tiles, 16, LANES), BF16), vmem((state_tiles, 16, LANES), BF16),
        vmem((state_tiles, 16, LANES), F32), vmem((state_tiles, 16, LANES), BF16),
        vmem((lane_rows, LANES), F32), vmem((lane_rows, LANES), F32),
        vmem((8, LANES), F32), vmem((chips + 1, 8, LANES), F32),
        vmem((tiles, 8, LANES), F32), square, square, vmem((2, rows, LANES), F32),
        square, square, square, vmem((16, LANES), F32),
        vmem((part_tiles, 8, LANES), F32), vmem((8, channels), F32), vmem((16, channels), F32),
        vmem((8, channels), F32), vmem((n, part_tiles // n, 8, LANES), F32),
        pltpu.SemaphoreType.DMA((2,)), pltpu.SemaphoreType.DMA((4, n)),
        *states(F32), *states(BF16),
    ]
    whole = pl.BlockSpec(memory_space=pltpu.VMEM)
    normed, grad_xbc, grad_z, gdt, sums = pl.pallas_call(
        functools.partial(whole_kernel, n, axis),
        out_shape=[
            jax.ShapeDtypeStruct((rows, inner), BF16), jax.ShapeDtypeStruct((rows, channels), BF16),
            jax.ShapeDtypeStruct((rows, inner), BF16), jax.ShapeDtypeStruct((rows, LANES), F32),
            jax.ShapeDtypeStruct((part_tiles, 8, LANES), F32),
        ],
        in_specs=[whole] * 7,
        out_specs=[whole] * 5,
        scratch_shapes=scratch,
        compiler_params=pltpu.CompilerParams(vmem_limit_bytes=VMEM_LIMIT, collective_id=1, has_side_effects=True),
    )(xbc_raw, gate_z, dt, alog, conv_weight, norm_gain[None], grad_out)
    conv_total = sums[: tiles + 1, :4].transpose(1, 0, 2).reshape(4, channels)
    return (
        normed, grad_xbc, grad_z, gdt[:, :heads], conv_total,
        sums[tiles, 4, :heads], sums[:tiles, 4].reshape(inner),
    )


def solution(mesh):
    split = P(("groups", "context"), None)
    return jax.shard_map(
        on_device,
        mesh=mesh,
        in_specs=(split, split, split, P(), P(), P(), split),
        out_specs=(split, split, split, split, P("groups", None), P("groups"), P("groups")),
        check_vma=False,
    )
```

```python
import functools
import math

import jax
import jax.numpy as jnp
from jax import lax
from jax.experimental import pallas as pl
from jax.experimental.pallas import tpu as pltpu
from jax.sharding import PartitionSpec as P

HEADDIM = 64
DSTATE = 64
LANES = 128
MESH = pl.DeviceIdType.MESH
F32 = jnp.float32
BF16 = jnp.bfloat16
VMEM_LIMIT = 48 * 1024 * 1024


def dot(a, b, ca=1, cb=0):
    return lax.dot_general(a, b, (((ca,), (cb,)), ((), ())), preferred_element_type=F32)


def dot_exact(a, b):
    return jnp.dot(a, b, precision=lax.Precision.HIGHEST, preferred_element_type=F32)


def iota(shape, axis):
    return lax.broadcasted_iota(jnp.int32, shape, axis)


def tile_at(k):
    return pl.ds(pl.multiple_of(k * LANES, LANES), LANES)


def conv_pre(x, halo, taps):
    ext = jnp.concatenate([halo, x], axis=0)
    rows = x.shape[0]
    return ext, sum(taps[o : o + 1] * ext[5 + o : 5 + o + rows] for o in range(4))


def sigmoid(v):
    return 1.0 / (1.0 + jnp.exp(-v))


def steps_of(dt_ref, alog_ref, run_t, step_t):
    raw = dt_ref[...]
    step = jnp.maximum(raw, 0.0) + jnp.log1p(jnp.exp(-jnp.abs(raw)))
    log_decay = -jnp.exp(alog_ref[0:1]) * step
    rows = raw.shape[0]
    tri = (iota((rows, rows), 0) >= iota((rows, rows), 1)).astype(F32)
    running = dot_exact(tri, log_decay)
    run_t[...] = running.T
    step_t[...] = step.T
    return step, log_decay, running


def columns_of(row_ref, k):
    low = jnp.broadcast_to(row_ref[pl.ds(2 * k, 1), :], (LANES, LANES))
    high = jnp.broadcast_to(row_ref[pl.ds(2 * k + 1, 1), :], (LANES, LANES))
    low_t, high_t = low.T, high.T
    return low, high, low_t, high_t, jnp.where(iota((LANES, LANES), 1) < HEADDIM, low_t, high_t)


def pair_weights(run_t, step_t, k):
    low, high, low_t, high_t, _ = columns_of(run_t, k)
    causal = iota((LANES, LANES), 0) >= iota((LANES, LANES), 1)
    gaps = [jnp.where(causal, a - b, -1e30) for a, b in ((low_t, low), (high_t, high))]
    scaled = [jnp.exp(gap) * step_t[pl.ds(2 * k + i, 1), :] for i, gap in enumerate(gaps)]
    return jnp.concatenate(scaled, axis=0)


def projections(bc):
    lane = iota(bc.shape, 1)
    turned = pltpu.roll(bc.astype(F32), HEADDIM, 1)
    b_low = jnp.where(lane < DSTATE, bc.astype(F32), 0.0).astype(BF16)
    c_low = jnp.where(lane < DSTATE, turned, 0.0).astype(BF16)
    b_high = jnp.where(lane >= DSTATE, turned, 0.0).astype(BF16)
    return b_low, c_low, b_high


def head_sum(value, k):
    pick = (iota((LANES, LANES), 1) == 2 * k + iota((LANES, LANES), 0) // HEADDIM).astype(BF16)
    high = value.astype(BF16)
    return dot(high, pick) + dot((value - high.astype(F32)).astype(BF16), pick)


def state_tile(ref, k):
    return ref[pl.ds(4 * k, 4)].reshape(DSTATE, LANES)


def forward_part(x_ref, halo_ref, w_ref, run_t, step_t, mix_ref, end_ref, lanes_ref, grown, to_ends):
    tiles = x_ref.shape[1] // LANES - 1
    lanes_ref[...] = jnp.zeros_like(lanes_ref)

    def mixin(k):
        at = tile_at(k)
        _, pre = conv_pre(x_ref[:, at].astype(F32), halo_ref[:, at], w_ref[:, at])
        mixed = (pre * sigmoid(pre)).astype(BF16)
        mix_ref[:, at] = mixed
        return mixed

    bc = mixin(tiles)

    def body(k, carry):
        mixed = mixin(k)
        spread = columns_of(run_t, k)[-1]
        to_end = jnp.exp(spread[-1:] - spread) * columns_of(step_t, k)[-1]
        grown[:, tile_at(k)] = jnp.exp(spread)
        to_ends[:, tile_at(k)] = to_end
        lanes_ref[pl.ds(k, 1), :] = spread[-1:]
        ended = dot(bc, (mixed.astype(F32) * to_end).astype(BF16), 0, 0)
        end_ref[pl.ds(4 * k, 4)] = ended[:DSTATE].reshape(4, 16, LANES).astype(BF16)
        return carry

    lax.fori_loop(0, tiles, body, 0, unroll=2)
    spare = end_ref.shape[0] - 4 * tiles
    if spare:
        end_ref[4 * tiles :] = jnp.zeros((spare, 16, LANES), BF16)


def scores_of(bc):
    b_low, c_low, b_high = projections(bc)
    scores = dot(c_low, b_low, 1, 1)
    return b_low, c_low, b_high, jnp.concatenate([scores, scores], axis=0)


def within_part(begin, end, mix_ref, scores2, run_t, step_t, mixer, scaled_ref):
    lane = iota((LANES, LANES), 1)

    def body(k, carry):
        at = tile_at(k)
        scaled = pair_weights(run_t, step_t, k)
        scaled_ref[k] = scaled
        both = dot((scores2[...] * scaled).astype(BF16), mix_ref[:, at])
        mixer[:, at] = jnp.where(lane < HEADDIM, both[:LANES], both[LANES:])
        return carry

    lax.fori_loop(begin, end, body, 0, unroll=2)


def middle_part(
    mix_ref, z_ref, gain_ref, out_ref, start_ref, grown, mixer,
    normed_ref, gz_ref, gmix_ref, gstart_ref, gain_part_ref, along_ref, gc_ref, sums,
):
    inner = z_ref.shape[1]
    tiles = inner // LANES
    bc = mix_ref[:, inner : inner + LANES]
    _, c_low, _ = projections(bc)
    lane = iota((LANES, LANES), 1)
    c_both = jnp.where(lane < DSTATE, c_low.astype(F32), bc.astype(F32)).astype(BF16)

    def parts_of(k):
        start = state_tile(start_ref, k)
        high = start.astype(BF16)
        return jnp.concatenate([(start - high.astype(F32)).astype(BF16), high], axis=0)

    sums[...] = jnp.zeros_like(sums)

    def first(k, carry):
        at = tile_at(k)
        carried = dot(c_both, parts_of(k))
        mixed = mixer[:, at] + carried * grown[:, at]
        mixer[:, at] = mixed
        z = z_ref[:, at].astype(F32)
        gated = mixed * z * sigmoid(z)
        sums[0] += gated * gated
        sums[1] += gated * out_ref[:, at].astype(F32) * gain_ref[0:1, at]
        return carry

    lax.fori_loop(0, tiles, first, 0, unroll=2)
    scale = lax.rsqrt(jnp.sum(sums[0], axis=1, keepdims=True) / inner + 1e-05)
    back = scale * scale * scale * (jnp.sum(sums[1], axis=1, keepdims=True) / inner)
    along_ref[...] = jnp.zeros_like(along_ref)
    gc_ref[...] = jnp.zeros_like(gc_ref)

    def second(k, carry):
        at = tile_at(k)
        mixed = mixer[:, at]
        z = z_ref[:, at].astype(F32)
        gate = sigmoid(z)
        gated = mixed * z * gate
        gain = gain_ref[0:1, at]
        out = out_ref[:, at].astype(F32)
        plain = gated * scale
        normed_ref[:, at] = (plain * gain).astype(BF16)
        gain_row = jnp.sum(out * plain, axis=0, keepdims=True)
        gain_part_ref[k] = jnp.broadcast_to(gain_row, (8, LANES))
        ggated = out * gain * scale - gated * back
        gz_ref[:, at] = (ggated * mixed * gate * (1.0 + z * (1.0 - gate))).astype(BF16)
        exact = ggated * z * gate
        gmixer = exact.astype(BF16)
        gmix_ref[:, at] = exact
        wide = gmixer.astype(F32)
        along_ref[...] += head_sum(wide * mixed, k)
        decayed = exact * grown[:, at]
        high = decayed.astype(BF16)
        low = (decayed - high.astype(F32)).astype(BF16)
        placed = parts_of(k)
        gc_ref[...] += dot(high, placed, 1, 1) + dot(low, placed, 1, 1)
        started = dot(bc, high, 0, 0)
        gstart_ref[pl.ds(4 * k, 4)] = started[DSTATE:].reshape(4, 16, LANES).astype(BF16)
        return carry

    lax.fori_loop(0, tiles, second, 0, unroll=2)
    halves = gc_ref[...]
    gc_ref[...] = jnp.where(lane < DSTATE, 0.0, halves + pltpu.roll(halves, DSTATE, 1))
    spare = gstart_ref.shape[0] - 4 * tiles
    if spare:
        gstart_ref[4 * tiles :] = jnp.zeros((spare, 16, LANES), BF16)


def within_back(begin, end, mix_ref, gmix_ref, scores2, scaled_ref, gscores, gval, into):
    lane = iota((LANES, LANES), 1)

    def body(k, carry):
        at = tile_at(k)
        values = mix_ref[:, at]
        gmixer = gmix_ref[:, at]
        scaled = scaled_ref[k]
        weights = (scores2[...] * scaled).astype(BF16)
        wide = jnp.concatenate([jnp.where(lane < HEADDIM, gmixer, 0.0), jnp.where(lane < HEADDIM, 0.0, gmixer)], axis=0)
        split = wide.astype(BF16)
        rest = (wide - split.astype(F32)).astype(BF16)
        gweights = (dot(split, values, 1, 1) + dot(rest, values, 1, 1)) * scaled
        gscores[...] += gweights[:LANES] + gweights[LANES:]
        gvalues = dot(weights, split, 0, 0)
        into[...] += head_sum(values.astype(F32) * gvalues, k)
        gval[:, at] = gvalues
        return carry

    lax.fori_loop(begin, end, body, 0, unroll=2)


def backward_part(
    x_ref, halo_ref, mix_ref, dt_ref, alog_ref, w_ref, start_ref, gend_ref, gain_part_ref, along_ref, gbc,
    step_ref, decay_ref, grown, to_ends, gscores, gval, into, after, carry_rows,
    gx_ref, head_ref, tail_ref, gdt_ref, part_ref,
):
    inner = gval.shape[1]
    tiles = inner // LANES
    bc = mix_ref[:, inner : inner + LANES]
    _, c_low, b_high = projections(bc)
    blank = jnp.zeros((DSTATE, LANES), BF16)
    after[...] = jnp.zeros_like(after)
    carry_rows[...] = jnp.zeros_like(carry_rows)

    def conv_back(k, gmixin):
        at = tile_at(k)
        taps = w_ref[:, at]
        ext, pre = conv_pre(x_ref[:, at].astype(F32), halo_ref[:, at], taps)
        gate = sigmoid(pre)
        gpre = gmixin.astype(BF16).astype(F32) * gate * (1.0 + pre * (1.0 - gate))
        rows = gpre.shape[0]
        none = jnp.zeros((8, LANES), F32)
        padded = jnp.concatenate([none, gpre, none], axis=0)
        gext = sum(taps[o : o + 1] * padded[8 - o : 8 - o + rows + 8] for o in range(4))
        own = gext[3 : 3 + rows]
        gx_ref[:, at] = own.astype(BF16)
        tail_ref[:, at] = own[rows - 16 :]
        head_ref[:, at] = gext[:8]
        return [jnp.sum(gpre * ext[5 + o : 5 + o + rows], axis=0, keepdims=True) for o in range(4)]

    def body(k, carry):
        values = mix_ref[:, tile_at(k)]
        to_end = to_ends[:, tile_at(k)]
        start, gend = state_tile(start_ref, k), state_tile(gend_ref, k)
        gend_low = jnp.concatenate([gend, blank], axis=0)
        gended = to_end * dot(bc, gend_low)
        values32 = values.astype(F32)
        after[...] += head_sum(values32 * gended, k)
        moved = jnp.sum(start * gend.astype(F32), axis=0, keepdims=True) * grown[:, tile_at(k)][-1:]
        carry_rows[...] += head_sum(jnp.broadcast_to(moved, (16, LANES)), k)
        gbc[...] += dot((values32 * to_end).astype(BF16), gend_low, 1, 1)
        taps = conv_back(k, gval[:, tile_at(k)] + gended)
        part_ref[k] = jnp.concatenate(taps + [gain_part_ref[k][:1], jnp.zeros((3, LANES), F32)], axis=0)
        return carry

    lax.fori_loop(0, tiles, body, 0, unroll=2)
    gscore = gscores[...].astype(BF16)
    rest = (gscores[...] - gscore.astype(F32)).astype(BF16)
    from_scores = dot(gscore, c_low, 0, 0) + dot(gscore, b_high) + dot(rest, c_low, 0, 0) + dot(rest, b_high)
    taps = conv_back(tiles, gbc[...] + from_scores)
    step, log_decay = step_ref[...], decay_ref[...]
    rows = step.shape[0]
    later = (iota((rows, rows), 0) <= iota((rows, rows), 1)).astype(F32)
    earlier = (iota((rows, rows), 0) > iota((rows, rows), 1)).astype(F32)
    glog = dot_exact(later, along_ref[...] - into[...]) + dot_exact(earlier, after[...]) + carry_rows[0:1]
    gstep = (into[...] + after[...]) / step - jnp.exp(alog_ref[0:1]) * glog
    gdt_ref[...] = gstep * sigmoid(dt_ref[...])
    galog = jnp.sum(glog * log_decay, axis=0, keepdims=True)
    part_ref[tiles] = jnp.concatenate(taps + [galog, jnp.zeros((3, LANES), F32)], axis=0)
    spare = part_ref.shape[0] - tiles - 1
    if spare:
        part_ref[tiles + 1 :] = jnp.zeros((spare, 8, LANES), F32)


def greet_all(axis, n):
    me = lax.axis_index(axis)
    barrier = pltpu.get_barrier_semaphore()

    def greet(d, carry):
        pl.semaphore_signal(barrier, inc=1, device_id={axis: lax.rem(me + d, n)}, device_id_type=MESH)
        return carry

    lax.fori_loop(1, n, greet, 0)
    pl.semaphore_wait(barrier, n - 1)
    return me


def to_peer(src, dst, send_sem, recv_sem, axis, peer):
    return pltpu.make_async_remote_copy(
        src_ref=src, dst_ref=dst, send_sem=send_sem, recv_sem=recv_sem,
        device_id={axis: peer}, device_id_type=MESH,
    )


def over_peers(n, action):
    def one(d, carry):
        action(d)
        return carry

    lax.fori_loop(1, n, one, 0)


def exchange_part(
    n, axis, reverse, in_ref, lanes_ref, total_ref, out_ref, totals_ref, lanes_near,
    near, joined, held, decays, back, ret, passed, sems, meanwhile, finish,
):
    chips = n // 2
    me = lax.axis_index(axis)
    chip, core = lax.div(me, 2), lax.rem(me, 2)
    sibling = me + 1 - 2 * core
    half = in_ref.shape[0] // 2
    per = half // chips

    def peer(d):
        return 2 * lax.rem(chip + d + chips, chips) + core

    def block(j):
        return pl.ds(j * per, per)

    mine = core * half
    first = core == (1 if reverse else 0)
    swaps = [to_peer(in_ref.at[pl.ds((1 - core) * half, half)], near, sems.at[0, 0], sems.at[1, 0], axis, sibling)]
    if not reverse:
        swaps.append(to_peer(lanes_ref, lanes_near, sems.at[2, 0], sems.at[3, 0], axis, sibling))
        swaps.append(to_peer(total_ref, totals_ref.at[chips], sems.at[4, 0], sems.at[5, 0], axis, sibling))
    for swap in swaps:
        swap.start()
    for swap in swaps:
        swap.wait()

    def lane_decays(r):
        row = pl.ds(lax.div(mine, 4) + r, 1)
        return jnp.exp(lanes_ref[row, :]), jnp.exp(lanes_near[row, :])

    def join(r, carry):
        own, other = lane_decays(r)
        at = pl.ds(4 * r, 4)
        own_state = in_ref[pl.ds(mine + 4 * r, 4)].astype(F32)
        other_state = near[at].astype(F32)
        summed = own_state * jnp.where(first, other, 1.0) + other_state * jnp.where(first, 1.0, own)
        joined[at] = summed.astype(BF16)
        return carry

    lax.fori_loop(0, half // 4, join, 0)

    def outgoing(d):
        there = lax.rem(chip + d, chips)
        return to_peer(joined.at[block(there)], held.at[d], sems.at[0, d], sems.at[1, d], axis, peer(d))

    def totals_out(d):
        return to_peer(totals_ref.at[0], totals_ref.at[d], sems.at[2, d], sems.at[3, d], axis, peer(d))

    if not reverse:
        totals_ref[0] = total_ref[...] + totals_ref[chips]
        over_peers(chips, lambda d: totals_out(d).start())
    over_peers(chips, lambda d: outgoing(d).start())
    held[0] = joined[block(chip)]
    if not reverse:
        over_peers(chips, lambda d: totals_out(d).wait())
    logs = totals_ref[:chips].reshape(chips * 8, LANES)
    for i in range(per):
        pair = lax.div(mine + chip * per + i, 4)
        pick = iota((LANES, LANES), 0) == 2 * pair + iota((LANES, LANES), 1) // HEADDIM
        decays[:, i] = jnp.exp(dot_exact(logs, pick.astype(F32))).reshape(chips, 8, LANES)
    meanwhile()
    over_peers(chips, lambda d: outgoing(d).wait())

    def advance(step, state):
        j = chips - 1 - step if reverse else step
        d = lax.rem(chip - j + chips, chips)
        back[lax.rem(j - chip + chips, chips)] = state.astype(back.dtype)
        return decays[d][:, :1] * state + held[d].astype(F32)

    lax.fori_loop(0, chips, advance, jnp.zeros((per, 16, LANES), F32))

    def returning(d):
        return to_peer(back.at[d], ret.at[block(chip)], sems.at[4, d], sems.at[5, d], axis, peer(d))

    def arriving(d):
        there = lax.rem(chip - d + chips, chips)
        return to_peer(back.at[d], ret.at[block(there)], sems.at[4, d], sems.at[5, d], axis, peer(-d))

    over_peers(chips, lambda d: returning(d).start())
    ret[block(chip)] = back[0]
    finish()
    over_peers(chips, lambda d: returning(d).wait_send())
    over_peers(chips, lambda d: arriving(d).wait_recv())

    def hand(r, carry):
        own, other = lane_decays(r)
        at = pl.ds(4 * r, 4)
        own_state = in_ref[pl.ds(mine + 4 * r, 4)].astype(F32)
        other_state = near[at].astype(F32)
        begun = ret[at].astype(F32)
        moved = jnp.where(first, own, other) * begun + jnp.where(first, own_state, other_state)
        out_ref[pl.ds(mine + 4 * r, 4)] = jnp.where(first, begun, moved).astype(out_ref.dtype)
        passed[at] = jnp.where(first, moved, begun).astype(passed.dtype)
        return carry

    lax.fori_loop(0, half // 4, hand, 0)
    final = to_peer(passed, out_ref.at[pl.ds(mine, half)], sems.at[6, 0], sems.at[7, 0], axis, sibling)
    final.start()
    final.wait_send()
    to_peer(passed, out_ref.at[pl.ds((1 - core) * half, half)], sems.at[6, 0], sems.at[7, 0], axis, sibling).wait_recv()


def total_part(n, axis, part_ref, head_ref, out_ref, rows_ref, held, sems):
    me = lax.axis_index(axis)
    per = part_ref.shape[0] // n

    def block(j):
        return pl.ds(j * per, per)

    def outgoing(d):
        return to_peer(part_ref.at[block(lax.rem(me + d, n))], held.at[d], sems.at[0, d], sems.at[1, d], axis, lax.rem(me + d, n))

    over_peers(n, lambda d: outgoing(d).start())
    rim = to_peer(head_ref, rows_ref, sems.at[2, 0], sems.at[3, 0], axis, lax.rem(me + n - 1, n))
    rim.start()
    held[0] = part_ref[block(me)]
    over_peers(n, lambda d: outgoing(d).wait())

    def add(d, total):
        return total + held[d]

    held[0] = lax.fori_loop(1, n, add, held[0])
    out_ref[block(me)] = held[0]

    def returning(d):
        return to_peer(held.at[0], out_ref.at[block(me)], sems.at[2, d], sems.at[3, d], axis, lax.rem(me + d, n))

    def arriving(d):
        source = lax.rem(me - d + n, n)
        return to_peer(held.at[0], out_ref.at[block(source)], sems.at[2, d], sems.at[3, d], axis, source)

    over_peers(n, lambda d: returning(d).start())
    over_peers(n, lambda d: returning(d).wait_send())
    over_peers(n, lambda d: arriving(d).wait_recv())
    rim.wait()


def whole_kernel(
    n, axis,
    x_ref, z_ref, dt_ref, alog_ref, w_ref, gain_ref, out_ref,
    normed_ref, gx_ref, gz_ref, gdt_ref, sums_ref,
    rim, halo, run_t, step_t, step_ref, decay_ref, mix, scores2, mixer, gmix, gval,
    ended, gstart, start, gend, lanes, lanes_near, total, totals,
    gain_part, along, gc, norm_sums, gscores, into, after, carry_rows,
    part, head, tail, back_rows, grown, to_ends, scaled, z_held, out_held, fetch_sems, total_held, rim_sems, total_sems, *states,
):
    rows, inner = z_ref.shape
    tiles = inner // LANES
    middle = tiles // 4 * 2
    fetches = [
        pltpu.make_async_copy(z_ref, z_held, fetch_sems.at[0]),
        pltpu.make_async_copy(out_ref, out_held, fetch_sems.at[1]),
    ]
    for fetch in fetches:
        fetch.start()
    me = greet_all(axis, n)
    last = to_peer(x_ref.at[rows - 16 :], rim, rim_sems.at[0], rim_sems.at[1], axis, lax.rem(me + 1, n))
    last.start()
    step, log_decay, running = steps_of(dt_ref, alog_ref, run_t, step_t)
    step_ref[...] = step
    decay_ref[...] = log_decay
    total[...] = jnp.broadcast_to(running[-1:], total.shape)
    last.wait()
    halo[...] = jnp.where(me > 0, rim[...].astype(F32)[8:], 0.0)
    forward_part(x_ref, halo, w_ref, run_t, step_t, mix, ended, lanes, grown, to_ends)
    scores2[...] = scores_of(mix[:, inner : inner + LANES])[3]

    def within(begin, end):
        return lambda: within_part(begin, end, mix, scores2, run_t, step_t, mixer, scaled)

    exchange_part(
        n, axis, False, ended, lanes, total, start, totals, lanes_near, *states[:8],
        within(0, middle), within(middle, tiles),
    )
    for fetch in fetches:
        fetch.wait()
    middle_part(
        mix, z_held, gain_ref, out_held, start, grown, mixer,
        normed_ref, gz_ref, gmix, gstart, gain_part, along, gc, norm_sums,
    )
    gscores[...] = jnp.zeros_like(gscores)
    into[...] = jnp.zeros_like(into)

    def back(begin, end):
        return lambda: within_back(begin, end, mix, gmix, scores2, scaled, gscores, gval, into)

    exchange_part(
        n, axis, True, gstart, lanes, None, gend, totals, lanes_near, *states[8:],
        back(0, middle), back(middle, tiles),
    )
    backward_part(
        x_ref, halo, mix, dt_ref, alog_ref, w_ref, start, gend, gain_part, along, gc,
        step_ref, decay_ref, grown, to_ends, gscores, gval, into, after, carry_rows,
        gx_ref, head, tail, gdt_ref, part,
    )
    total_part(n, axis, part, head, sums_ref, back_rows, total_held, total_sems)

    def mend(k, carry):
        at = tile_at(k)
        borrowed = jnp.where((iota((8, LANES), 0) < 3) & (me < n - 1), back_rows[:, at], 0.0)
        moved = jnp.concatenate([jnp.zeros((8, LANES), F32), pltpu.roll(borrowed, 5, 0)], axis=0)
        gx_ref[rows - 16 :, at] = (tail[:, at] + moved).astype(BF16)
        return carry

    lax.fori_loop(0, tiles + 1, mend, 0)


def on_device(xbc_raw, gate_z, dt_raw, a_log, conv_weight, norm_gain, grad_out):
    axis = "context"
    n = lax.axis_size(axis)
    rows, inner = gate_z.shape
    channels = xbc_raw.shape[1]
    heads = a_log.shape[0]
    tiles = inner // LANES
    unit = n * 8 // math.gcd(n, 8)
    state_tiles = -(-4 * tiles // unit) * unit
    lane_rows = -(-state_tiles // 32) * 8
    part_tiles = -(-(tiles + 1) // n) * n
    dt = jnp.pad(dt_raw, ((0, 0), (0, LANES - heads)))
    alog = jnp.pad(a_log, (0, LANES - heads))[None]
    chips, half = n // 2, state_tiles // 2
    per = half // chips
    vmem = pltpu.VMEM
    square = vmem((rows, LANES), F32)
    wide = vmem((rows, inner), F32)

    def states(kept):
        return [
            vmem((half, 16, LANES), BF16), vmem((half, 16, LANES), BF16), vmem((chips, per, 16, LANES), BF16),
            vmem((chips, per, 8, LANES), F32), vmem((chips, per, 16, LANES), kept),
            vmem((half, 16, LANES), kept), vmem((half, 16, LANES), kept), pltpu.SemaphoreType.DMA((8, chips)),
        ]

    scratch = [
        vmem((16, channels), BF16), vmem((8, channels), F32), vmem((LANES, rows), F32), vmem((LANES, rows), F32),
        square, square, vmem((rows, channels), BF16), vmem((2 * rows, LANES), F32), wide, wide, wide,
        vmem((state_tiles, 16, LANES), BF16), vmem((state_tiles, 16, LANES), BF16),
        vmem((state_tiles, 16, LANES), F32), vmem((state_tiles, 16, LANES), BF16),
        vmem((lane_rows, LANES), F32), vmem((lane_rows, LANES), F32),
        vmem((8, LANES), F32), vmem((chips + 1, 8, LANES), F32),
        vmem((tiles, 8, LANES), F32), square, square, vmem((2, rows, LANES), F32),
        square, square, square, vmem((16, LANES), F32),
        vmem((part_tiles, 8, LANES), F32), vmem((8, channels), F32), vmem((16, channels), F32),
        vmem((8, channels), F32), wide, wide, vmem((tiles, 2 * rows, LANES), F32),
        vmem((rows, inner), BF16), vmem((rows, inner), BF16), pltpu.SemaphoreType.DMA((2,)),
        vmem((n, part_tiles // n, 8, LANES), F32),
        pltpu.SemaphoreType.DMA((2,)), pltpu.SemaphoreType.DMA((4, n)),
        *states(F32), *states(BF16),
    ]
    whole = pl.BlockSpec(memory_space=pltpu.VMEM)
    away = pl.BlockSpec(memory_space=pl.ANY)
    normed, grad_xbc, grad_z, gdt, sums = pl.pallas_call(
        functools.partial(whole_kernel, n, axis),
        out_shape=[
            jax.ShapeDtypeStruct((rows, inner), BF16), jax.ShapeDtypeStruct((rows, channels), BF16),
            jax.ShapeDtypeStruct((rows, inner), BF16), jax.ShapeDtypeStruct((rows, LANES), F32),
            jax.ShapeDtypeStruct((part_tiles, 8, LANES), F32),
        ],
        in_specs=[whole, away, whole, whole, whole, whole, away],
        out_specs=[whole] * 5,
        scratch_shapes=scratch,
        compiler_params=pltpu.CompilerParams(vmem_limit_bytes=VMEM_LIMIT, collective_id=1, has_side_effects=True),
    )(xbc_raw, gate_z, dt, alog, conv_weight, norm_gain[None], grad_out)
    conv_total = sums[: tiles + 1, :4].transpose(1, 0, 2).reshape(4, channels)
    return (
        normed, grad_xbc, grad_z, gdt[:, :heads], conv_total,
        sums[tiles, 4, :heads], sums[:tiles, 4].reshape(inner),
    )


def solution(mesh):
    split = P(("groups", "context"), None)
    return jax.shard_map(
        on_device,
        mesh=mesh,
        in_specs=(split, split, split, P(), P(), P(), split),
        out_specs=(split, split, split, split, P("groups", None), P("groups"), P("groups")),
        check_vma=False,
    )
```

```python
import functools
import math

import jax
import jax.numpy as jnp
from jax import lax
from jax.experimental import pallas as pl
from jax.experimental.pallas import tpu as pltpu
from jax.sharding import PartitionSpec as P

HEADDIM = 64
DSTATE = 64
LANES = 128
MESH = pl.DeviceIdType.MESH
F32 = jnp.float32
BF16 = jnp.bfloat16
VMEM_LIMIT = 60 * 1024 * 1024


def dot(a, b, ca=1, cb=0):
    return lax.dot_general(a, b, (((ca,), (cb,)), ((), ())), preferred_element_type=F32)


def dot_exact(a, b):
    return jnp.dot(a, b, precision=lax.Precision.HIGHEST, preferred_element_type=F32)


def iota(shape, axis):
    return lax.broadcasted_iota(jnp.int32, shape, axis)


def tile_at(k):
    return pl.ds(pl.multiple_of(k * LANES, LANES), LANES)


def conv_pre(x, halo, taps):
    ext = jnp.concatenate([halo, x], axis=0)
    rows = x.shape[0]
    return ext, sum(taps[o : o + 1] * ext[5 + o : 5 + o + rows] for o in range(4))


def sigmoid(v):
    return 1.0 / (1.0 + jnp.exp(-v))


def steps_of(dt_ref, alog_ref, run_t, step_t):
    raw = dt_ref[...]
    step = jnp.maximum(raw, 0.0) + jnp.log1p(jnp.exp(-jnp.abs(raw)))
    log_decay = -jnp.exp(alog_ref[0:1]) * step
    rows = raw.shape[0]
    tri = (iota((rows, rows), 0) >= iota((rows, rows), 1)).astype(F32)
    running = dot_exact(tri, log_decay)
    run_t[...] = running.T
    step_t[...] = step.T
    return step, log_decay, running


def columns_of(row_ref, k):
    low = jnp.broadcast_to(row_ref[pl.ds(2 * k, 1), :], (LANES, LANES))
    high = jnp.broadcast_to(row_ref[pl.ds(2 * k + 1, 1), :], (LANES, LANES))
    low_t, high_t = low.T, high.T
    return low, high, low_t, high_t, jnp.where(iota((LANES, LANES), 1) < HEADDIM, low_t, high_t)


def pair_weights(run_t, step_t, k):
    low, high, low_t, high_t, _ = columns_of(run_t, k)
    causal = iota((LANES, LANES), 0) >= iota((LANES, LANES), 1)
    gaps = [jnp.where(causal, a - b, -1e30) for a, b in ((low_t, low), (high_t, high))]
    scaled = [jnp.exp(gap) * step_t[pl.ds(2 * k + i, 1), :] for i, gap in enumerate(gaps)]
    return jnp.concatenate(scaled, axis=0)


def projections(bc):
    lane = iota(bc.shape, 1)
    turned = pltpu.roll(bc.astype(F32), HEADDIM, 1)
    b_low = jnp.where(lane < DSTATE, bc.astype(F32), 0.0).astype(BF16)
    c_low = jnp.where(lane < DSTATE, turned, 0.0).astype(BF16)
    b_high = jnp.where(lane >= DSTATE, turned, 0.0).astype(BF16)
    return b_low, c_low, b_high


def head_sum(value, k):
    pick = (iota((LANES, LANES), 1) == 2 * k + iota((LANES, LANES), 0) // HEADDIM).astype(BF16)
    high = value.astype(BF16)
    return dot(high, pick) + dot((value - high.astype(F32)).astype(BF16), pick)


def state_tile(ref, k):
    return ref[pl.ds(4 * k, 4)].reshape(DSTATE, LANES)


def forward_part(x_ref, halo_ref, w_ref, run_t, step_t, mix_ref, end_ref, lanes_ref, grown, to_ends):
    tiles = x_ref.shape[1] // LANES - 1
    lanes_ref[...] = jnp.zeros_like(lanes_ref)

    def mixin(k):
        at = tile_at(k)
        _, pre = conv_pre(x_ref[:, at].astype(F32), halo_ref[:, at], w_ref[:, at])
        mixed = (pre * sigmoid(pre)).astype(BF16)
        mix_ref[:, at] = mixed
        return mixed

    bc = mixin(tiles)

    def body(k, carry):
        mixed = mixin(k)
        spread = columns_of(run_t, k)[-1]
        to_end = jnp.exp(spread[-1:] - spread) * columns_of(step_t, k)[-1]
        grown[:, tile_at(k)] = jnp.exp(spread)
        to_ends[:, tile_at(k)] = to_end
        lanes_ref[pl.ds(k, 1), :] = spread[-1:]
        ended = dot(bc, (mixed.astype(F32) * to_end).astype(BF16), 0, 0)
        end_ref[pl.ds(4 * k, 4)] = ended[:DSTATE].reshape(4, 16, LANES).astype(BF16)
        return carry

    lax.fori_loop(0, tiles, body, 0, unroll=2)
    spare = end_ref.shape[0] - 4 * tiles
    if spare:
        end_ref[4 * tiles :] = jnp.zeros((spare, 16, LANES), BF16)


def scores_of(bc):
    b_low, c_low, b_high = projections(bc)
    scores = dot(c_low, b_low, 1, 1)
    return b_low, c_low, b_high, jnp.concatenate([scores, scores], axis=0)


def within_part(begin, end, mix_ref, scores2, run_t, step_t, mixer, scaled_ref):
    lane = iota((LANES, LANES), 1)

    def body(k, carry):
        at = tile_at(k)
        scaled = pair_weights(run_t, step_t, k)
        scaled_ref[k] = scaled
        both = dot((scores2[...] * scaled).astype(BF16), mix_ref[:, at])
        mixer[:, at] = jnp.where(lane < HEADDIM, both[:LANES], both[LANES:])
        return carry

    lax.fori_loop(begin, end, body, 0, unroll=2)


def middle_part(
    mix_ref, z_ref, gain_ref, out_ref, start_ref, grown, mixer,
    normed_ref, gz_ref, gmix_ref, gstart_ref, gain_part_ref, along_ref, gc_ref, sums,
):
    inner = z_ref.shape[1]
    tiles = inner // LANES
    bc = mix_ref[:, inner : inner + LANES]
    _, c_low, _ = projections(bc)
    lane = iota((LANES, LANES), 1)
    c_both = jnp.where(lane < DSTATE, c_low.astype(F32), bc.astype(F32)).astype(BF16)

    def parts_of(k):
        start = state_tile(start_ref, k)
        high = start.astype(BF16)
        return jnp.concatenate([(start - high.astype(F32)).astype(BF16), high], axis=0)

    sums[...] = jnp.zeros_like(sums)

    def first(k, carry):
        at = tile_at(k)
        carried = dot(c_both, parts_of(k))
        mixed = mixer[:, at] + carried * grown[:, at]
        mixer[:, at] = mixed
        z = z_ref[:, at].astype(F32)
        gated = mixed * z * sigmoid(z)
        sums[0] += gated * gated
        sums[1] += gated * out_ref[:, at].astype(F32) * gain_ref[0:1, at]
        return carry

    lax.fori_loop(0, tiles, first, 0, unroll=2)
    scale = lax.rsqrt(jnp.sum(sums[0], axis=1, keepdims=True) / inner + 1e-05)
    back = scale * scale * scale * (jnp.sum(sums[1], axis=1, keepdims=True) / inner)
    along_ref[...] = jnp.zeros_like(along_ref)
    gc_ref[...] = jnp.zeros_like(gc_ref)

    def second(k, carry):
        at = tile_at(k)
        mixed = mixer[:, at]
        z = z_ref[:, at].astype(F32)
        gate = sigmoid(z)
        gated = mixed * z * gate
        gain = gain_ref[0:1, at]
        out = out_ref[:, at].astype(F32)
        plain = gated * scale
        normed_ref[:, at] = (plain * gain).astype(BF16)
        gain_row = jnp.sum(out * plain, axis=0, keepdims=True)
        gain_part_ref[k] = jnp.broadcast_to(gain_row, (8, LANES))
        ggated = out * gain * scale - gated * back
        gz_ref[:, at] = (ggated * mixed * gate * (1.0 + z * (1.0 - gate))).astype(BF16)
        exact = ggated * z * gate
        gmixer = exact.astype(BF16)
        gmix_ref[:, at] = exact
        wide = gmixer.astype(F32)
        along_ref[...] += head_sum(wide * mixed, k)
        decayed = exact * grown[:, at]
        high = decayed.astype(BF16)
        low = (decayed - high.astype(F32)).astype(BF16)
        placed = parts_of(k)
        gc_ref[...] += dot(high, placed, 1, 1) + dot(low, placed, 1, 1)
        started = dot(bc, high, 0, 0)
        gstart_ref[pl.ds(4 * k, 4)] = started[DSTATE:].reshape(4, 16, LANES).astype(BF16)
        return carry

    lax.fori_loop(0, tiles, second, 0, unroll=2)
    halves = gc_ref[...]
    gc_ref[...] = jnp.where(lane < DSTATE, 0.0, halves + pltpu.roll(halves, DSTATE, 1))
    spare = gstart_ref.shape[0] - 4 * tiles
    if spare:
        gstart_ref[4 * tiles :] = jnp.zeros((spare, 16, LANES), BF16)


def within_back(begin, end, mix_ref, gmix_ref, scores2, scaled_ref, gscores, gval, into):
    lane = iota((LANES, LANES), 1)

    def body(k, carry):
        at = tile_at(k)
        values = mix_ref[:, at]
        gmixer = gmix_ref[:, at]
        scaled = scaled_ref[k]
        weights = (scores2[...] * scaled).astype(BF16)
        wide = jnp.concatenate([jnp.where(lane < HEADDIM, gmixer, 0.0), jnp.where(lane < HEADDIM, 0.0, gmixer)], axis=0)
        split = wide.astype(BF16)
        rest = (wide - split.astype(F32)).astype(BF16)
        gweights = (dot(split, values, 1, 1) + dot(rest, values, 1, 1)) * scaled
        gscores[...] += gweights[:LANES] + gweights[LANES:]
        gvalues = dot(weights, split, 0, 0)
        into[...] += head_sum(values.astype(F32) * gvalues, k)
        gval[:, at] = gvalues
        return carry

    lax.fori_loop(begin, end, body, 0, unroll=2)


def backward_part(
    x_ref, halo_ref, mix_ref, dt_ref, alog_ref, w_ref, start_ref, gend_ref, gain_part_ref, along_ref, gbc,
    step_ref, decay_ref, grown, to_ends, gscores, gval, into, after, carry_rows,
    gx_ref, head_ref, tail_ref, gdt_ref, part_ref,
):
    inner = gval.shape[1]
    tiles = inner // LANES
    bc = mix_ref[:, inner : inner + LANES]
    _, c_low, b_high = projections(bc)
    blank = jnp.zeros((DSTATE, LANES), BF16)
    after[...] = jnp.zeros_like(after)
    carry_rows[...] = jnp.zeros_like(carry_rows)

    def conv_back(k, gmixin):
        at = tile_at(k)
        taps = w_ref[:, at]
        ext, pre = conv_pre(x_ref[:, at].astype(F32), halo_ref[:, at], taps)
        gate = sigmoid(pre)
        gpre = gmixin.astype(BF16).astype(F32) * gate * (1.0 + pre * (1.0 - gate))
        rows = gpre.shape[0]
        none = jnp.zeros((8, LANES), F32)
        padded = jnp.concatenate([none, gpre, none], axis=0)
        gext = sum(taps[o : o + 1] * padded[8 - o : 8 - o + rows + 8] for o in range(4))
        own = gext[3 : 3 + rows]
        gx_ref[:, at] = own.astype(BF16)
        tail_ref[:, at] = own[rows - 16 :]
        head_ref[:, at] = gext[:8]
        return [jnp.sum(gpre * ext[5 + o : 5 + o + rows], axis=0, keepdims=True) for o in range(4)]

    def body(k, carry):
        values = mix_ref[:, tile_at(k)]
        to_end = to_ends[:, tile_at(k)]
        start, gend = state_tile(start_ref, k), state_tile(gend_ref, k)
        gend_low = jnp.concatenate([gend, blank], axis=0)
        gended = to_end * dot(bc, gend_low)
        values32 = values.astype(F32)
        after[...] += head_sum(values32 * gended, k)
        moved = jnp.sum(start * gend.astype(F32), axis=0, keepdims=True) * grown[:, tile_at(k)][-1:]
        carry_rows[...] += head_sum(jnp.broadcast_to(moved, (16, LANES)), k)
        gbc[...] += dot((values32 * to_end).astype(BF16), gend_low, 1, 1)
        taps = conv_back(k, gval[:, tile_at(k)] + gended)
        part_ref[k] = jnp.concatenate(taps + [gain_part_ref[k][:1], jnp.zeros((3, LANES), F32)], axis=0)
        return carry

    lax.fori_loop(0, tiles, body, 0, unroll=2)
    gscore = gscores[...].astype(BF16)
    rest = (gscores[...] - gscore.astype(F32)).astype(BF16)
    from_scores = dot(gscore, c_low, 0, 0) + dot(gscore, b_high) + dot(rest, c_low, 0, 0) + dot(rest, b_high)
    taps = conv_back(tiles, gbc[...] + from_scores)
    step, log_decay = step_ref[...], decay_ref[...]
    rows = step.shape[0]
    later = (iota((rows, rows), 0) <= iota((rows, rows), 1)).astype(F32)
    earlier = (iota((rows, rows), 0) > iota((rows, rows), 1)).astype(F32)
    glog = dot_exact(later, along_ref[...] - into[...]) + dot_exact(earlier, after[...]) + carry_rows[0:1]
    gstep = (into[...] + after[...]) / step - jnp.exp(alog_ref[0:1]) * glog
    gdt_ref[...] = gstep * sigmoid(dt_ref[...])
    galog = jnp.sum(glog * log_decay, axis=0, keepdims=True)
    part_ref[tiles] = jnp.concatenate(taps + [galog, jnp.zeros((3, LANES), F32)], axis=0)
    spare = part_ref.shape[0] - tiles - 1
    if spare:
        part_ref[tiles + 1 :] = jnp.zeros((spare, 8, LANES), F32)


def greet_all(axis, n):
    me = lax.axis_index(axis)
    barrier = pltpu.get_barrier_semaphore()

    def greet(d, carry):
        pl.semaphore_signal(barrier, inc=1, device_id={axis: lax.rem(me + d, n)}, device_id_type=MESH)
        return carry

    lax.fori_loop(1, n, greet, 0)
    pl.semaphore_wait(barrier, n - 1)
    return me


def to_peer(src, dst, send_sem, recv_sem, axis, peer):
    return pltpu.make_async_remote_copy(
        src_ref=src, dst_ref=dst, send_sem=send_sem, recv_sem=recv_sem,
        device_id={axis: peer}, device_id_type=MESH,
    )


def over_peers(n, action):
    def one(d, carry):
        action(d)
        return carry

    lax.fori_loop(1, n, one, 0)


def exchange_part(
    n, axis, reverse, in_ref, lanes_ref, total_ref, out_ref, totals_ref, lanes_near,
    near, joined, held, decays, back, ret, passed, sems, meanwhile, finish,
):
    chips = n // 2
    me = lax.axis_index(axis)
    chip, core = lax.div(me, 2), lax.rem(me, 2)
    sibling = me + 1 - 2 * core
    half = in_ref.shape[0] // 2
    per = half // chips

    def peer(d):
        return 2 * lax.rem(chip + d + chips, chips) + core

    def block(j):
        return pl.ds(j * per, per)

    mine = core * half
    first = core == (1 if reverse else 0)
    swaps = [to_peer(in_ref.at[pl.ds((1 - core) * half, half)], near, sems.at[0, 0], sems.at[1, 0], axis, sibling)]
    if not reverse:
        swaps.append(to_peer(lanes_ref, lanes_near, sems.at[2, 0], sems.at[3, 0], axis, sibling))
        swaps.append(to_peer(total_ref, totals_ref.at[chips], sems.at[4, 0], sems.at[5, 0], axis, sibling))
    for swap in swaps:
        swap.start()
    for swap in swaps:
        swap.wait()

    def lane_decays(r):
        row = pl.ds(lax.div(mine, 4) + r, 1)
        return jnp.exp(lanes_ref[row, :]), jnp.exp(lanes_near[row, :])

    def join(r, carry):
        own, other = lane_decays(r)
        at = pl.ds(4 * r, 4)
        own_state = in_ref[pl.ds(mine + 4 * r, 4)].astype(F32)
        other_state = near[at].astype(F32)
        summed = own_state * jnp.where(first, other, 1.0) + other_state * jnp.where(first, 1.0, own)
        joined[at] = summed.astype(BF16)
        return carry

    lax.fori_loop(0, half // 4, join, 0)

    def outgoing(d):
        there = lax.rem(chip + d, chips)
        return to_peer(joined.at[block(there)], held.at[d], sems.at[0, d], sems.at[1, d], axis, peer(d))

    def totals_out(d):
        return to_peer(totals_ref.at[0], totals_ref.at[d], sems.at[2, d], sems.at[3, d], axis, peer(d))

    if not reverse:
        totals_ref[0] = total_ref[...] + totals_ref[chips]
        over_peers(chips, lambda d: totals_out(d).start())
    over_peers(chips, lambda d: outgoing(d).start())
    held[0] = joined[block(chip)]
    if not reverse:
        over_peers(chips, lambda d: totals_out(d).wait())
    logs = totals_ref[:chips].reshape(chips * 8, LANES)
    for i in range(per):
        pair = lax.div(mine + chip * per + i, 4)
        pick = iota((LANES, LANES), 0) == 2 * pair + iota((LANES, LANES), 1) // HEADDIM
        decays[:, i] = jnp.exp(dot_exact(logs, pick.astype(F32))).reshape(chips, 8, LANES)
    meanwhile()
    over_peers(chips, lambda d: outgoing(d).wait())

    def advance(step, state):
        j = chips - 1 - step if reverse else step
        d = lax.rem(chip - j + chips, chips)
        back[lax.rem(j - chip + chips, chips)] = state.astype(back.dtype)
        return decays[d][:, :1] * state + held[d].astype(F32)

    lax.fori_loop(0, chips, advance, jnp.zeros((per, 16, LANES), F32))

    def returning(d):
        return to_peer(back.at[d], ret.at[block(chip)], sems.at[4, d], sems.at[5, d], axis, peer(d))

    def arriving(d):
        there = lax.rem(chip - d + chips, chips)
        return to_peer(back.at[d], ret.at[block(there)], sems.at[4, d], sems.at[5, d], axis, peer(-d))

    over_peers(chips, lambda d: returning(d).start())
    ret[block(chip)] = back[0]
    finish()
    over_peers(chips, lambda d: returning(d).wait_send())
    over_peers(chips, lambda d: arriving(d).wait_recv())

    def hand(r, carry):
        own, other = lane_decays(r)
        at = pl.ds(4 * r, 4)
        own_state = in_ref[pl.ds(mine + 4 * r, 4)].astype(F32)
        other_state = near[at].astype(F32)
        begun = ret[at].astype(F32)
        moved = jnp.where(first, own, other) * begun + jnp.where(first, own_state, other_state)
        out_ref[pl.ds(mine + 4 * r, 4)] = jnp.where(first, begun, moved).astype(out_ref.dtype)
        passed[at] = jnp.where(first, moved, begun).astype(passed.dtype)
        return carry

    lax.fori_loop(0, half // 4, hand, 0)
    final = to_peer(passed, out_ref.at[pl.ds(mine, half)], sems.at[6, 0], sems.at[7, 0], axis, sibling)
    final.start()
    final.wait_send()
    to_peer(passed, out_ref.at[pl.ds((1 - core) * half, half)], sems.at[6, 0], sems.at[7, 0], axis, sibling).wait_recv()


def total_part(n, axis, part_ref, head_ref, out_ref, rows_ref, held, sems):
    me = lax.axis_index(axis)
    per = part_ref.shape[0] // n

    def block(j):
        return pl.ds(j * per, per)

    def outgoing(d):
        return to_peer(part_ref.at[block(lax.rem(me + d, n))], held.at[d], sems.at[0, d], sems.at[1, d], axis, lax.rem(me + d, n))

    over_peers(n, lambda d: outgoing(d).start())
    rim = to_peer(head_ref, rows_ref, sems.at[2, 0], sems.at[3, 0], axis, lax.rem(me + n - 1, n))
    rim.start()
    held[0] = part_ref[block(me)]
    over_peers(n, lambda d: outgoing(d).wait())

    def add(d, total):
        return total + held[d]

    held[0] = lax.fori_loop(1, n, add, held[0])
    out_ref[block(me)] = held[0]

    def returning(d):
        return to_peer(held.at[0], out_ref.at[block(me)], sems.at[2, d], sems.at[3, d], axis, lax.rem(me + d, n))

    def arriving(d):
        source = lax.rem(me - d + n, n)
        return to_peer(held.at[0], out_ref.at[block(source)], sems.at[2, d], sems.at[3, d], axis, source)

    over_peers(n, lambda d: returning(d).start())
    over_peers(n, lambda d: returning(d).wait_send())
    over_peers(n, lambda d: arriving(d).wait_recv())
    rim.wait()


def whole_kernel(
    n, axis,
    x_ref, z_ref, dt_ref, alog_ref, w_ref, gain_ref, out_ref,
    normed_ref, gx_ref, gz_ref, gdt_ref, sums_ref,
    rim, halo, run_t, step_t, step_ref, decay_ref, mix, scores2, mixer, gmix, gval,
    ended, gstart, start, gend, lanes, lanes_near, total, totals,
    gain_part, along, gc, norm_sums, gscores, into, after, carry_rows,
    part, head, tail, back_rows, grown, to_ends, scaled, z_held, out_held, fetch_sems, total_held, rim_sems, total_sems, *states,
):
    rows, inner = z_ref.shape
    tiles = inner // LANES
    middle = tiles // 4 * 2
    fetches = [
        pltpu.make_async_copy(z_ref, z_held, fetch_sems.at[0]),
        pltpu.make_async_copy(out_ref, out_held, fetch_sems.at[1]),
    ]
    for fetch in fetches:
        fetch.start()
    me = greet_all(axis, n)
    last = to_peer(x_ref.at[rows - 16 :], rim, rim_sems.at[0], rim_sems.at[1], axis, lax.rem(me + 1, n))
    last.start()
    step, log_decay, running = steps_of(dt_ref, alog_ref, run_t, step_t)
    step_ref[...] = step
    decay_ref[...] = log_decay
    total[...] = jnp.broadcast_to(running[-1:], total.shape)
    last.wait()
    halo[...] = jnp.where(me > 0, rim[...].astype(F32)[8:], 0.0)
    forward_part(x_ref, halo, w_ref, run_t, step_t, mix, ended, lanes, grown, to_ends)
    scores2[...] = scores_of(mix[:, inner : inner + LANES])[3]

    def within(begin, end):
        return lambda: within_part(begin, end, mix, scores2, run_t, step_t, mixer, scaled)

    exchange_part(
        n, axis, False, ended, lanes, total, start, totals, lanes_near, *states[:8],
        within(0, middle), within(middle, tiles),
    )
    for fetch in fetches:
        fetch.wait()
    middle_part(
        mix, z_held, gain_ref, out_held, start, grown, mixer,
        normed_ref, gz_ref, gmix, gstart, gain_part, along, gc, norm_sums,
    )
    gscores[...] = jnp.zeros_like(gscores)
    into[...] = jnp.zeros_like(into)

    def back(begin, end):
        return lambda: within_back(begin, end, mix, gmix, scores2, scaled, gscores, gval, into)

    exchange_part(
        n, axis, True, gstart, lanes, None, gend, totals, lanes_near, *states[8:],
        back(0, middle), back(middle, tiles),
    )
    backward_part(
        x_ref, halo, mix, dt_ref, alog_ref, w_ref, start, gend, gain_part, along, gc,
        step_ref, decay_ref, grown, to_ends, gscores, gval, into, after, carry_rows,
        gx_ref, head, tail, gdt_ref, part,
    )
    total_part(n, axis, part, head, sums_ref, back_rows, total_held, total_sems)

    def mend(k, carry):
        at = tile_at(k)
        borrowed = jnp.where((iota((8, LANES), 0) < 3) & (me < n - 1), back_rows[:, at], 0.0)
        moved = jnp.concatenate([jnp.zeros((8, LANES), F32), pltpu.roll(borrowed, 5, 0)], axis=0)
        gx_ref[rows - 16 :, at] = (tail[:, at] + moved).astype(BF16)
        return carry

    lax.fori_loop(0, tiles + 1, mend, 0)


def on_device(xbc_raw, gate_z, dt_raw, a_log, conv_weight, norm_gain, grad_out):
    axis = "context"
    n = lax.axis_size(axis)
    rows, inner = gate_z.shape
    channels = xbc_raw.shape[1]
    heads = a_log.shape[0]
    tiles = inner // LANES
    unit = n * 8 // math.gcd(n, 8)
    state_tiles = -(-4 * tiles // unit) * unit
    lane_rows = -(-state_tiles // 32) * 8
    part_tiles = -(-(tiles + 1) // n) * n
    dt = jnp.pad(dt_raw, ((0, 0), (0, LANES - heads)))
    alog = jnp.pad(a_log, (0, LANES - heads))[None]
    chips, half = n // 2, state_tiles // 2
    per = half // chips
    vmem = pltpu.VMEM
    square = vmem((rows, LANES), F32)
    wide = vmem((rows, inner), F32)

    def states(kept):
        return [
            vmem((half, 16, LANES), BF16), vmem((half, 16, LANES), BF16), vmem((chips, per, 16, LANES), BF16),
            vmem((chips, per, 8, LANES), F32), vmem((chips, per, 16, LANES), kept),
            vmem((half, 16, LANES), kept), vmem((half, 16, LANES), kept), pltpu.SemaphoreType.DMA((8, chips)),
        ]

    scratch = [
        vmem((16, channels), BF16), vmem((8, channels), F32), vmem((LANES, rows), F32), vmem((LANES, rows), F32),
        square, square, vmem((rows, channels), BF16), vmem((2 * rows, LANES), F32), wide, wide, wide,
        vmem((state_tiles, 16, LANES), BF16), vmem((state_tiles, 16, LANES), BF16),
        vmem((state_tiles, 16, LANES), F32), vmem((state_tiles, 16, LANES), BF16),
        vmem((lane_rows, LANES), F32), vmem((lane_rows, LANES), F32),
        vmem((8, LANES), F32), vmem((chips + 1, 8, LANES), F32),
        vmem((tiles, 8, LANES), F32), square, square, vmem((2, rows, LANES), F32),
        square, square, square, vmem((16, LANES), F32),
        vmem((part_tiles, 8, LANES), F32), vmem((8, channels), F32), vmem((16, channels), F32),
        vmem((8, channels), F32), wide, wide, vmem((tiles, 2 * rows, LANES), F32),
        vmem((rows, inner), BF16), vmem((rows, inner), BF16), pltpu.SemaphoreType.DMA((2,)),
        vmem((n, part_tiles // n, 8, LANES), F32),
        pltpu.SemaphoreType.DMA((2,)), pltpu.SemaphoreType.DMA((4, n)),
        *states(F32), *states(BF16),
    ]
    whole = pl.BlockSpec(memory_space=pltpu.VMEM)
    away = pl.BlockSpec(memory_space=pl.ANY)
    normed, grad_xbc, grad_z, gdt, sums = pl.pallas_call(
        functools.partial(whole_kernel, n, axis),
        out_shape=[
            jax.ShapeDtypeStruct((rows, inner), BF16), jax.ShapeDtypeStruct((rows, channels), BF16),
            jax.ShapeDtypeStruct((rows, inner), BF16), jax.ShapeDtypeStruct((rows, LANES), F32),
            jax.ShapeDtypeStruct((part_tiles, 8, LANES), F32),
        ],
        in_specs=[whole, away, whole, whole, whole, whole, away],
        out_specs=[whole] * 5,
        scratch_shapes=scratch,
        compiler_params=pltpu.CompilerParams(vmem_limit_bytes=VMEM_LIMIT, collective_id=1, has_side_effects=True),
    )(xbc_raw, gate_z, dt, alog, conv_weight, norm_gain[None], grad_out)
    conv_total = sums[: tiles + 1, :4].transpose(1, 0, 2).reshape(4, channels)
    return (
        normed, grad_xbc, grad_z, gdt[:, :heads], conv_total,
        sums[tiles, 4, :heads], sums[:tiles, 4].reshape(inner),
    )


def solution(mesh):
    split = P(("groups", "context"), None)
    return jax.shard_map(
        on_device,
        mesh=mesh,
        in_specs=(split, split, split, P(), P(), P(), split),
        out_specs=(split, split, split, split, P("groups", None), P("groups"), P("groups")),
        check_vma=False,
    )
```
